32 devices in a mesh: pool: 1, fsdp: 32 (over z, y, x, core).
Axes of the slice: x: 2, y: 2, z: 4, core: 2. Of those that a mesh axis runs over, the one named last changes fastest.
Arguments:
- noisy: bfloat16 [2048, 2560], P(('pool', 'fsdp')), may hold values from -6 to 6
- clean: bfloat16 [2048, 2560], P(('pool', 'fsdp')), may hold values from -6 to 6
- seg_ids: int32 [32], P('pool'), may hold values from 0 to 3, never falling along the last dimension, each value on 1 to 12 neighbouring positions
- lag_mask: int32 [32, 2], P(('pool', 'fsdp')), may hold values 0 or 1
- plan: int32 [32, 2], P(('pool', 'fsdp')), may hold values from 1 to 999, as said below
- w_query: bfloat16 [2560, 2560], P('fsdp'), may hold values from -0.125 to 0.125
- w_key: bfloat16 [2560, 2560], P('fsdp'), may hold values from -0.125 to 0.125
- time_proj: bfloat16 [128, 7680], replicated, may hold values from -0.5 to 0.5
- q_gain: float32 [2560], replicated, may hold values from 0.5 to 14
- k_gain: float32 [2560], replicated, may hold values from 0.5 to 14
Outputs:
- denoised: bfloat16 [2048, 2560], P(('pool', 'fsdp'))
The draws below stay inside these ranges and needn't reach their ends.
Inputs may be any that keep to these rules, and one draw needn't show every extreme that they name: seg_ids never falls along the spans; each rollout is 1 to 12 consecutive spans. `plan`: entry j of a row lies from 1000 * (1 - j) // 2 + 1 to 1000 * (2 - j) // 2 - 1, so each row falls strictly.
All inputs are finite; a program needn't handle non-finite values. No bound on the sum of `lag_mask` on one device may be relied on, other than what follows from the above.
Results may differ from the reference program's by a relative error of at most 0.024.
Values may be sent and summed in bfloat16 or wider, within the bound.
A program may use at most 128 MiB of HBM per device.

```python
import math
import jax
import jax.numpy as jnp
import numpy as np
from jax import lax

D = 2560
HEADS = 20
HEAD_DIM = 128
TIME_FEAT = 128
ROWS = 64
STEPS = 2
LAGS = 2
LEVELS = 1000
MOST_SPANS = 12
SPANS = 32
ROLLOUTS = 4


def draw_plan(key, part):
    columns = []
    for level_index in range(STEPS):
        lowest = LEVELS * (STEPS - 1 - level_index) // STEPS + 1
        highest = LEVELS * (STEPS - level_index) // STEPS
        columns.append(jax.random.randint(jax.random.fold_in(key, level_index), (SPANS, 1), lowest, highest))
    return jnp.concatenate(columns, axis=1).astype(jnp.int32)


def gain_law(key):
    total_width = HEADS * HEAD_DIM
    result = jnp.exp(jax.random.uniform(key, (total_width,), jnp.float32, math.log(0.5), math.log(2.0)))
    return result.astype(jnp.float32)


def draw_q_gain(key, part):
    return gain_law(jax.random.fold_in(key, 11))


def draw_k_gain(key, part):
    return gain_law(jax.random.fold_in(key, 23))


def plant(values, own_key, low, high):
    longest = values.shape.index(max(values.shape))
    spots = []
    for shift in (0, 1):
        where = [jax.random.randint(jax.random.fold_in(own_key, axis), (), 0, length) for axis, length in enumerate(values.shape)]
        where[longest] = (where[longest] + shift) % values.shape[longest]
        spots.append(tuple(where))
    return values.at[spots[0]].set(low).at[spots[1]].set(high)


def block_levels(rng, extent, split, smallest, largest):
    level = 1.0
    for dim, blocks in split:
        draws = jax.random.uniform(jax.random.fold_in(jax.random.fold_in(rng, 6), dim), (blocks,), jnp.float32, smallest / len(split), largest / len(split))
        level = level * jnp.repeat(jnp.exp(draws), extent[dim] // blocks).reshape((-1,) + (1,) * (len(extent) - 1 - dim))
    return level


def length_profile(amount, total, most, slope):
    loads = [(1 << 20) // math.isqrt(standing ** slope) + 1 for standing in range(2, amount + 1)]
    rest, holding = total - most - (amount - 1), [1] * (amount - 1)
    while rest > 0:
        candidates = [i for i in range(amount - 1) if holding[i] < most]
        whole, remaining = sum([loads[i] for i in candidates]), rest
        for i in candidates:
            extra = min(most - holding[i], max(1, remaining * loads[i] // whole), rest)
            holding[i] = holding[i] + extra
            rest = rest - extra
    return np.array([most] + holding)


def ragged_sizes(stream_key, number_of, total, limit, skew):
    if number_of == 2:
        one = jax.random.randint(stream_key, (), max(1, total - limit), min(limit, total - 1) + 1)
        return jnp.stack([one, total - one])
    tallies = jnp.asarray(length_profile(number_of, total, limit, skew), jnp.int32)
    pairs = (number_of - 1) // 2
    donor, taker = tallies[1:1 + 2 * pairs:2], tallies[2:2 + 2 * pairs:2]
    slack = jnp.minimum(donor - 1, limit - taker)
    moved = jax.random.randint(jax.random.fold_in(stream_key, 1), (pairs,), 0, 1 << 20) % (slack + 1)
    tallies = tallies.at[1:1 + 2 * pairs:2].set(donor - moved).at[2:2 + 2 * pairs:2].set(taker + moved)
    return tallies[jax.random.permutation(jax.random.fold_in(stream_key, 2), number_of)]


def noise(key, extent, width, most, shards=(), kind=jnp.bfloat16):
    values = width * jax.random.normal(key, extent, jnp.float32)
    if shards:
        values = values * block_levels(key, extent, shards, -0.22, 0.18)
    return jnp.clip(values, -most, most).astype(kind)


def setup_inputs(seed: int = 0, part: int = 0) -> dict:
    splits = jax.random.split(jax.random.key(seed), 11)
    part_splits = jax.random.split(jax.random.fold_in(splits[10], part), 11)
    return {
        "noisy": noise(part_splits[0], (SPANS * ROWS, D), 1.0, 6.0, ((0, 32),)),
        "clean": noise(part_splits[1], (SPANS * ROWS, D), 1.0, 6.0, ((0, 32),)),
        "seg_ids": jnp.searchsorted(jnp.cumsum(ragged_sizes(part_splits[2], ROLLOUTS, SPANS, MOST_SPANS, 1)), jnp.arange(SPANS), side="right").astype(jnp.int32),
        "lag_mask": plant((jax.random.randint(part_splits[3], (SPANS, LAGS), 0, 4) < 3).astype(jnp.int32), jax.random.fold_in(part_splits[3], 1), 0, 1),
        "plan": draw_plan(jax.random.fold_in(jax.random.fold_in(splits[10], part), 71), part),
        "w_query": noise(splits[5], (D, HEADS * HEAD_DIM), D ** -0.5, 0.125, ((0, 32),)),
        "w_key": noise(splits[6], (D, HEADS * HEAD_DIM), D ** -0.5, 0.125, ((0, 32),)),
        "time_proj": noise(splits[7], (TIME_FEAT, 3 * D), TIME_FEAT ** -0.5, 0.5),
        "q_gain": draw_q_gain(jax.random.fold_in(splits[10], 71), part),
        "k_gain": draw_k_gain(jax.random.fold_in(splits[10], 71), part),
    }


SIGMA_SHIFT = 5.0
EPSILON = 1e-06
MASKED = -1e+30

def sigma_of(levels):
    fraction = levels.astype(jnp.float32) / LEVELS
    return SIGMA_SHIFT * fraction / (1.0 + (SIGMA_SHIFT - 1.0) * fraction)

def frequencies(half_count):
    return jnp.exp(-math.log(10000.0) * jnp.arange(half_count, dtype=jnp.float32) / half_count)

def modulation(sigmas, time_proj):
    half_count = time_proj.shape[0] // 2
    angles = 1000.0 * sigmas[:, None] * frequencies(half_count)[None, :]
    features = jnp.concatenate([jnp.cos(angles), jnp.sin(angles)], axis=1).astype(jnp.bfloat16)
    return jnp.dot(features, time_proj, preferred_element_type=jnp.float32)

def modulate(latent, shift_row, scale_row):
    values = latent.astype(jnp.float32)
    centred = values - lax.optimization_barrier(jnp.mean(values, axis=-1, keepdims=True))
    variance = lax.optimization_barrier(jnp.mean(centred * centred, axis=-1, keepdims=True))
    normed = centred * lax.rsqrt(variance + EPSILON)
    return (normed * (1.0 + scale_row) + shift_row).astype(jnp.bfloat16)

def normalize(values, gain):
    mean_square = lax.optimization_barrier(jnp.mean(values * values, axis=-1, keepdims=True))
    return values * lax.rsqrt(mean_square + EPSILON) * gain

def rotate(values, positions):
    half_count = HEAD_DIM // 2
    split_heads = values.reshape(values.shape[:-1] + (HEADS, HEAD_DIM))
    angles = positions[..., None] * frequencies(half_count)
    cosine = jnp.cos(angles)[..., None, :]
    sine = jnp.sin(angles)[..., None, :]
    front = split_heads[..., :half_count]
    back = split_heads[..., half_count:]
    turned = jnp.concatenate([front * cosine - back * sine, front * sine + back * cosine], axis=-1)
    return turned.reshape(values.shape)

def attend(operands):
    query_rows, key_rows, value_rows, usable = operands
    row_count = query_rows.shape[0]
    query_heads = query_rows.astype(jnp.float32).reshape(row_count, HEADS, HEAD_DIM)
    key_heads = key_rows.astype(jnp.float32).reshape(-1, HEADS, HEAD_DIM)
    value_heads = value_rows.astype(jnp.float32).reshape(-1, HEADS, HEAD_DIM)
    scores = jnp.einsum('qhd,khd->hqk', query_heads, key_heads) * HEAD_DIM ** (-0.5)
    scores = jnp.where(usable[None, None, :], scores, MASKED)
    highest = lax.optimization_barrier(jnp.max(scores, axis=-1, keepdims=True))
    expanded = jnp.exp(scores - highest)
    weights = (expanded / lax.optimization_barrier(jnp.sum(expanded, axis=-1, keepdims=True))).astype(jnp.bfloat16)
    mixed = jnp.einsum('hqk,khd->qhd', weights.astype(jnp.float32), value_heads)
    return mixed.reshape(row_count, HEADS * HEAD_DIM).astype(jnp.bfloat16)

def reference(noisy, clean, seg_ids, lag_mask, plan, w_query, w_key, time_proj, q_gain, k_gain):
    span_count = seg_ids.shape[0]
    order = jnp.arange(span_count, dtype=jnp.int32)
    segment_start = lax.optimization_barrier(jnp.sum((seg_ids[None, :] < seg_ids[:, None]).astype(jnp.int32), axis=1))
    span_place = order - segment_start
    positions = (span_place[:, None] * ROWS + jnp.arange(ROWS, dtype=jnp.int32)[None, :]).astype(jnp.float32)
    rest_mod = modulation(jnp.zeros((1,), jnp.float32), time_proj)[0]
    context_hidden = modulate(clean, rest_mod[:D], rest_mod[D:2 * D])
    context_key = rotate(normalize(jnp.dot(context_hidden, w_key, preferred_element_type=jnp.float32), k_gain).reshape(span_count, ROWS, -1), positions).astype(jnp.bfloat16)
    context_value = context_hidden.reshape(span_count, ROWS, -1)
    lag_keys = []
    lag_values = []
    usable_parts = [jnp.ones((span_count, ROWS), jnp.int32) > 0]
    for distance in range(1, LAGS + 1):
        source = jnp.maximum(order - distance, 0)
        allowed = (order >= distance) & (seg_ids[source] == seg_ids) & (lag_mask[:, distance - 1] == 1)
        lag_keys.append(context_key[source])
        lag_values.append(context_value[source])
        usable_parts.append(jnp.broadcast_to(allowed[:, None], (span_count, ROWS)))
    keys_context = jnp.concatenate(lag_keys, axis=1)
    values_context = jnp.concatenate(lag_values, axis=1)
    usable = jnp.concatenate(usable_parts, axis=1)
    sigmas = [sigma_of(plan[:, level_index]) for level_index in range(STEPS)] + [jnp.zeros((span_count,), jnp.float32)]
    latent = noisy
    for step_index in range(STEPS):
        mod_rows = modulation(sigmas[step_index], time_proj)
        current = latent.reshape(span_count, ROWS, D)
        hidden = modulate(current, mod_rows[:, None, :D], mod_rows[:, None, D:2 * D])
        flat_hidden = hidden.reshape(span_count * ROWS, D)
        query_all = rotate(normalize(jnp.dot(flat_hidden, w_query, preferred_element_type=jnp.float32), q_gain).reshape(span_count, ROWS, -1), positions).astype(jnp.bfloat16)
        key_all = rotate(normalize(jnp.dot(flat_hidden, w_key, preferred_element_type=jnp.float32), k_gain).reshape(span_count, ROWS, -1), positions).astype(jnp.bfloat16)
        keys_joined = jnp.concatenate([key_all, keys_context], axis=1)
        values_joined = jnp.concatenate([hidden, values_context], axis=1)
        mixed = lax.map(attend, (query_all, keys_joined, values_joined, usable))
        sigma_change = sigmas[step_index + 1] - sigmas[step_index]
        factor = sigma_change[:, None, None] * mod_rows[:, None, 2 * D:]
        latent = (current.astype(jnp.float32) + factor * mixed.astype(jnp.float32)).astype(jnp.bfloat16).reshape(span_count * ROWS, D)
    return latent
```

```python
import functools
import math

import jax
import jax.numpy as jnp
from jax import lax
from jax.experimental import pallas as pl
from jax.experimental.pallas import tpu as pltpu
from jax.sharding import PartitionSpec as P

HEADS = 20
HEAD_DIM = 128
STEPS = 2
LAGS = 2
LEVELS = 1000


SIGMA_SHIFT = 5.0
EPSILON = 1e-06
MASKED = -1e30


def passed_along(value, axis, steps):
    count = lax.axis_size(axis)
    leading, last = (max(0, -steps), min(count, count - steps))
    return lax.ppermute(value, axis, [(source, source + steps) for source in range(leading, last)])


def sigma_of(levels):
    fraction = levels.astype(jnp.float32) / LEVELS
    return SIGMA_SHIFT * fraction / (1.0 + (SIGMA_SHIFT - 1.0) * fraction)


def frequencies(half_count):
    return jnp.exp(-math.log(10000.0) * jnp.arange(half_count, dtype=jnp.float32) / half_count)


def modulation(sigmas, time_proj):
    half_count = time_proj.shape[0] // 2
    angles = 1000.0 * sigmas[:, None] * frequencies(half_count)[None, :]
    features = jnp.concatenate([jnp.cos(angles), jnp.sin(angles)], axis=1).astype(jnp.bfloat16)
    return jnp.dot(features, time_proj, preferred_element_type=jnp.float32)[0]


def modulate(latent, mod_row, model_width):
    values = latent.astype(jnp.float32)
    centred = values - jnp.mean(values, axis=-1, keepdims=True)
    variance = jnp.mean(centred * centred, axis=-1, keepdims=True)
    normed = centred * lax.rsqrt(variance + EPSILON)
    return (normed * (1.0 + mod_row[model_width : 2 * model_width]) + mod_row[:model_width]).astype(
        jnp.bfloat16
    )


def normalize(values, gain):
    mean_square = jnp.mean(values * values, axis=-1, keepdims=True)
    return values * lax.rsqrt(mean_square + EPSILON) * gain


def rotate(values, positions):
    half_count = HEAD_DIM // 2
    split_heads = values.reshape(values.shape[:-1] + (HEADS, HEAD_DIM))
    angles = positions[..., None] * frequencies(half_count)
    cosine = jnp.cos(angles)[..., None, :]
    sine = jnp.sin(angles)[..., None, :]
    front = split_heads[..., :half_count]
    back = split_heads[..., half_count:]
    turned = jnp.concatenate([front * cosine - back * sine, front * sine + back * cosine], axis=-1)
    return turned.reshape(values.shape)


def attend(query_rows, key_rows, value_rows, usable):
    row_count = query_rows.shape[0]
    query_heads = query_rows.reshape(row_count, HEADS, HEAD_DIM)
    key_heads = key_rows.reshape(-1, HEADS, HEAD_DIM)
    value_heads = value_rows.reshape(-1, HEADS, HEAD_DIM)
    scores = jnp.einsum(
        "qhd,khd->hqk", query_heads, key_heads, preferred_element_type=jnp.float32
    ) * HEAD_DIM ** (-0.5)
    scores = jnp.where(usable[None, None, :], scores, MASKED)
    highest = jnp.max(scores, axis=-1, keepdims=True)
    expanded = jnp.exp(scores - highest)
    weights = (expanded / jnp.sum(expanded, axis=-1, keepdims=True)).astype(jnp.bfloat16)
    mixed = jnp.einsum("hqk,khd->qhd", weights, value_heads, preferred_element_type=jnp.float32)
    return mixed.reshape(row_count, HEADS * HEAD_DIM).astype(jnp.bfloat16)


def make_absorbers(noisy_hidden, context_hidden):

    def absorb_both(carry, pieces, offset):
        stored = tuple((piece_rows for piece_rows in pieces))
        query_sum = jnp.dot(noisy_hidden, pieces[0], preferred_element_type=jnp.float32)
        key_sum = jnp.dot(noisy_hidden, pieces[1], preferred_element_type=jnp.float32)
        ctxkey_sum = jnp.dot(context_hidden, pieces[1], preferred_element_type=jnp.float32)
        return (stored, (query_sum, key_sum, ctxkey_sum))

    def absorb_key(carry, piece, offset):
        buffer_rows, partials = carry
        stored = lax.dynamic_update_slice_in_dim(buffer_rows, piece, offset, 0)
        key_sum, ctxkey_sum = partials
        key_sum = key_sum + jnp.dot(noisy_hidden, piece, preferred_element_type=jnp.float32)
        ctxkey_sum = ctxkey_sum + jnp.dot(context_hidden, piece, preferred_element_type=jnp.float32)
        return (stored, (key_sum, ctxkey_sum))

    def absorb_query(carry, piece, offset):
        buffer_rows, query_sum = carry
        stored = lax.dynamic_update_slice_in_dim(buffer_rows, piece, offset, 0)
        query_sum = query_sum + jnp.dot(noisy_hidden, piece, preferred_element_type=jnp.float32)
        return (stored, query_sum)

    return (absorb_both, absorb_key, absorb_query)


def local(noisy, clean, seg_ids, lag_mask, plan, w_query, w_key, time_proj, q_gain, k_gain):
    row_count, model_width = noisy.shape
    inner_width = w_query.shape[1]
    span_index = lax.axis_index("fsdp")
    segment_start = jnp.sum((seg_ids < seg_ids[span_index]).astype(jnp.int32))
    span_place = span_index - segment_start
    positions = (span_place * row_count + jnp.arange(row_count, dtype=jnp.int32)).astype(
        jnp.float32
    )
    sigmas = [sigma_of(plan[0, level_index : level_index + 1]) for level_index in range(STEPS)] + [
        jnp.zeros((1,), jnp.float32)
    ]
    rest_mod = modulation(jnp.zeros((1,), jnp.float32), time_proj)
    step_mods = [modulation(sigmas[level_index], time_proj) for level_index in range(STEPS)]
    context_hidden = modulate(clean, rest_mod, model_width)
    noisy_hidden = modulate(noisy, step_mods[0], model_width)
    absorb_both, absorb_key, absorb_query = make_absorbers(noisy_hidden, context_hidden)
    empty_buffer = jnp.zeros((model_width, inner_width), jnp.bfloat16)
    empty_sum = jnp.zeros((row_count, inner_width), jnp.float32)
    buffers, partials = absorb_both(
        ((empty_buffer, empty_buffer), (empty_sum, empty_sum, empty_sum)),
        (
            lax.all_gather(w_query, "fsdp", axis=0, tiled=True),
            lax.all_gather(w_key, "fsdp", axis=0, tiled=True),
        ),
        jnp.int32(0),
    )
    full_query, full_key = buffers
    query_sum, key_sum, ctxkey_sum = partials
    context_key = rotate(normalize(ctxkey_sum, k_gain), positions).astype(jnp.bfloat16)
    context_pair = jnp.stack([context_key, context_hidden])
    received = [passed_along(context_pair, "fsdp", 1)]
    distance = 2
    received.append(passed_along(context_pair, "fsdp", distance))
    usable_parts = [jnp.ones((row_count,), jnp.int32) > 0]
    for distance in range(1, LAGS + 1):
        source = jnp.maximum(span_index - distance, 0)
        allowed = (
            (span_index >= distance)
            & (seg_ids[source] == seg_ids[span_index])
            & (lag_mask[0, distance - 1] == 1)
        )
        usable_parts.append(jnp.broadcast_to(allowed, (row_count,)))
    usable = jnp.concatenate(usable_parts)
    keys_context = jnp.concatenate([pair_rows[0] for pair_rows in received], axis=0)
    values_context = jnp.concatenate([pair_rows[1] for pair_rows in received], axis=0)
    latent = noisy
    for step_index in range(STEPS):
        if step_index == 0:
            hidden = noisy_hidden
            query_raw, key_raw = (query_sum, key_sum)
        else:
            hidden = modulate(latent, step_mods[step_index], model_width)
            query_raw = jnp.dot(hidden, full_query, preferred_element_type=jnp.float32)
            key_raw = jnp.dot(hidden, full_key, preferred_element_type=jnp.float32)
        query_rows = rotate(normalize(query_raw, q_gain), positions).astype(jnp.bfloat16)
        key_rows = rotate(normalize(key_raw, k_gain), positions).astype(jnp.bfloat16)
        mixed = attend(
            query_rows,
            jnp.concatenate([key_rows, keys_context], axis=0),
            jnp.concatenate([hidden, values_context], axis=0),
            usable,
        )
        sigma_change = sigmas[step_index + 1] - sigmas[step_index]
        factor = sigma_change * step_mods[step_index][2 * model_width :]
        latent = (latent.astype(jnp.float32) + factor[None, :] * mixed.astype(jnp.float32)).astype(
            jnp.bfloat16
        )
    return latent


TEAM = 4
MESH = pl.DeviceIdType.MESH


def fused_kernel(
    count, bias_ref, feat_ref, sig_ref, cos_ref, sin_ref, noisy_ref, clean_ref, wq_ref, wk_ref,
    proj_ref, qg_ref, kg_ref, out_ref,
    w_all, hid, hid2, ctx_k, ctx_v, qk_raw, ck_raw, stat, mix, mix_out, latent, mods, q_rows, k_rows,
    bias_all, send_sem, recv_sem, local_sem,
):
    rows, width = noisy_ref.shape
    part = wq_ref.shape[0]
    inner = wq_ref.shape[1] // TEAM
    heads = inner // HEAD_DIM
    groups = count // TEAM
    half = groups // 2
    me = lax.axis_index("fsdp")
    group = me // TEAM
    rank = me % TEAM
    sib_rank = rank + 1 - 2 * (rank % 2)
    far_rank = (rank + 2) % TEAM
    diag_rank = (sib_rank + 2) % TEAM
    ranks = [rank, sib_rank, far_rank, diag_rank]
    low = group % 2
    spot = group // 2 + low * (groups - 1 - 2 * (group // 2))

    def group_at(place):
        place = (place + 2 * groups) % groups
        upper = place // half
        return 2 * (place + upper * (groups - 1 - 2 * place)) + upper

    base = group * TEAM
    peers = [base + r for r in ranks]
    ring_next = group_at(spot + 1) * TEAM + rank
    ring_prev = group_at(spot - 1) * TEAM + rank
    later = ((group + 1) % groups) * TEAM + rank
    earlier = ((group + groups - 1) % groups) * TEAM + rank

    def cols(r):
        return pl.ds(pl.multiple_of(r * inner, 128), inner)

    def wrows(device):
        return pl.ds(pl.multiple_of(device * part, 16), part)

    barrier = pltpu.get_barrier_semaphore()
    friends = peers[1:] + [ring_next, ring_prev, later, earlier]
    for friend in friends:
        pl.semaphore_signal(barrier, inc=1, device_id={"fsdp": friend}, device_id_type=MESH)

    own = [
        pltpu.make_async_copy(
            ref.at[:, cols(rank)], w_all.at[wrows(me), pl.ds(k * inner, inner)], local_sem.at[k]
        )
        for k, ref in enumerate((wq_ref, wk_ref))
    ]
    for copy in own:
        copy.start()
    for copy in own:
        copy.wait()
    pl.semaphore_wait(barrier, len(friends))

    used = [0]
    started = []

    def remote(src, dst, target):
        index = used[0]
        used[0] += 1
        copy = pltpu.make_async_remote_copy(
            src_ref=src, dst_ref=dst, send_sem=send_sem.at[index], recv_sem=recv_sem.at[index],
            device_id={"fsdp": target}, device_id_type=MESH,
        )
        return copy, index

    def go(copy):
        copy[0].start()
        started.append(copy[0])

    def landing(copy, dst):
        return pltpu.make_async_remote_copy(
            src_ref=dst, dst_ref=dst, send_sem=send_sem.at[copy[1]],
            recv_sem=recv_sem.at[copy[1]], device_id={"fsdp": peers[1]}, device_id_type=MESH,
        )

    def ring_send(step, slot):
        arrivals = []
        for sign, target in ((1, ring_next), (-1, ring_prev)):
            lanes = pl.ds(0, 2 * inner)
            if step == half - 1:
                lanes = pl.ds(0, inner) if sign == 1 else pl.ds(inner, inner)
            source = group_at(spot - sign * step) * TEAM + ranks[slot]
            view = w_all.at[wrows(source), lanes]
            copy = remote(view, view, target)
            go(copy)
            coming = group_at(spot - sign * (step + 1)) * TEAM + ranks[slot]
            arrivals.append((copy, w_all.at[wrows(coming), lanes]))
        return arrivals

    ring = {}
    ring[0, 0] = ring_send(0, 0)
    scatter = {}
    for slot in range(1, TEAM):
        for k, ref in enumerate((wq_ref, wk_ref)):
            lanes = pl.ds(k * inner, inner)
            copy = remote(ref.at[:, cols(ranks[slot])], w_all.at[wrows(me), lanes], peers[slot])
            go(copy)
            scatter[slot, k] = (copy, w_all.at[wrows(peers[slot]), lanes])

    mods[...] = jnp.dot(feat_ref[...], proj_ref[...], preferred_element_type=jnp.float32)

    def modulated(values, index):
        centred = values - jnp.mean(values, axis=-1, keepdims=True)
        variance = jnp.mean(centred * centred, axis=-1, keepdims=True)
        normed = centred * lax.rsqrt(variance + EPSILON)
        scale = mods[index : index + 1, width : 2 * width]
        return (normed * (1.0 + scale) + mods[index : index + 1, :width]).astype(jnp.bfloat16)

    def share(buffer, lead):
        own_view = buffer.at[lead + (rank,)]
        to_sib = remote(own_view, own_view, peers[1])
        to_far = remote(own_view, own_view, peers[2])
        go(to_far)
        go(to_sib)
        return (
            landing(to_sib, buffer.at[lead + (sib_rank,)]),
            landing(to_far, buffer.at[lead + (far_rank,)]),
        )

    def share_rest(buffer, lead, pending):
        from_sib, from_far = pending
        from_far.wait_recv()
        view = buffer.at[lead + (far_rank,)]
        forward = remote(view, view, peers[1])
        go(forward)
        from_sib.wait_recv()
        landing(forward, buffer.at[lead + (diag_rank,)]).wait_recv()

    def share_all(buffer, lead):
        waits = []
        view = buffer.at[lead + (rank,)]
        for slot in (2, 3, 1):
            copy = remote(view, view, peers[slot])
            go(copy)
            waits.append(landing(copy, buffer.at[lead + (ranks[slot],)]))
        return waits

    latent[...] = noisy_ref[...].astype(jnp.float32)
    hid[0, pl.ds(rank, 1)] = modulated(latent[...], 1)[None]
    pending_noisy = share(hid, (0,))
    hid[1, pl.ds(rank, 1)] = modulated(clean_ref[...].astype(jnp.float32), 0)[None]
    pending_clean = share(hid, (1,))
    bias_all[pl.ds(rank, 1)] = bias_ref[...][None]
    pending_bias = share_all(bias_all, ())

    for slot in range(1, TEAM):
        for k in range(2):
            copy, view = scatter[slot, k]
            landing(copy, view).wait_recv()
        ring[0, slot] = ring_send(0, slot)

    share_rest(hid, (0,), pending_noisy)
    share_rest(hid, (1,), pending_clean)
    for wait in pending_bias:
        wait.wait_recv()

    for s in range(TEAM):
        ctx_v[LAGS + s] = hid[1, s, :, cols(rank)]
    v_copy = remote(ctx_v.at[pl.ds(TEAM, LAGS)], ctx_v.at[pl.ds(0, LAGS)], later)
    go(v_copy)

    for step in range(1, half):
        for slot in range(TEAM):
            for copy, view in ring[step - 1, slot]:
                landing(copy, view).wait_recv()
            ring[step, slot] = ring_send(step, slot)
    for slot in range(TEAM):
        for copy, view in ring[half - 1, slot]:
            landing(copy, view).wait_recv()
    landing(v_copy, ctx_v.at[pl.ds(0, LAGS)]).wait_recv()

    all_rows = TEAM * rows

    def project(source, first, last, target):
        start = first
        while start < last:
            size = min(256, last - start)
            target[:, start - first : start - first + size] = jnp.dot(
                source, w_all[:, start : start + size], preferred_element_type=jnp.float32
            )
            start += size

    ones = jnp.ones((8, inner), jnp.float32)
    nt = (((1,), (1,)), ((), ()))

    def squares(values):
        return lax.dot_general(
            ones, values * values, nt, precision=lax.Precision.HIGHEST,
            preferred_element_type=jnp.float32,
        )

    def row_scale(sums, index):
        pick = (lax.broadcasted_iota(jnp.int32, (8, 128), 0) == index).astype(jnp.float32)
        total = lax.dot_general(
            sums, pick, (((0,), (0,)), ((), ())), precision=lax.Precision.HIGHEST,
            preferred_element_type=jnp.float32,
        )
        return lax.rsqrt(total * (1.0 / width) + EPSILON)

    def turn(values, scale, gain_ref, h):
        gain = gain_ref[:, pl.ds(pl.multiple_of(rank * inner + h * HEAD_DIM, 128), HEAD_DIM)]
        value = values * scale * gain
        rolled = pltpu.roll(value, HEAD_DIM // 2, 1)
        return (value * cos_ref[...] + rolled * sin_ref[...]).astype(jnp.bfloat16)

    for step in range(STEPS):
        buffer = hid if step == 0 else hid2
        if step == 1:
            hid2[0, pl.ds(rank, 1)] = modulated(latent[...], 2)[None]
            share_rest(hid2, (0,), share(hid2, (0,)))
        rows_in = buffer[0].reshape(all_rows, width)
        project(rows_in, 0, 2 * inner, qk_raw)
        if step == 0:
            project(hid[1].reshape(all_rows, width), inner, 2 * inner, ck_raw)
        row_kind = lax.broadcasted_iota(jnp.int32, (8, all_rows), 0)
        sums = jnp.where(
            row_kind == 0, squares(qk_raw[:, :inner]), squares(qk_raw[:, inner:])
        )
        if step == 0:
            sums = jnp.where(row_kind == 2, squares(ck_raw[...]), sums)
        stat[step, pl.ds(rank, 1)] = sums[None]
        for wait in share_all(stat, (step,)):
            wait.wait_recv()
        total = stat[step, 0] + stat[step, 1] + stat[step, 2] + stat[step, 3]
        if step == 0:
            c_scale = row_scale(total, 2)
            for h in range(heads):
                lanes = slice(h * HEAD_DIM, (h + 1) * HEAD_DIM)
                turned = turn(ck_raw[:, lanes], c_scale, kg_ref, h)
                ctx_k[LAGS : LAGS + TEAM, :, lanes] = turned.reshape(TEAM, rows, HEAD_DIM)
            k_copy = remote(ctx_k.at[pl.ds(TEAM, LAGS)], ctx_k.at[pl.ds(0, LAGS)], later)
            go(k_copy)
        q_scale = row_scale(total, 0)
        k_scale = row_scale(total, 1)
        for h in range(heads):
            lanes = slice(h * HEAD_DIM, (h + 1) * HEAD_DIM)
            q_rows[:, lanes] = turn(qk_raw[:, lanes], q_scale, qg_ref, h)
            k_lanes = slice(inner + h * HEAD_DIM, inner + (h + 1) * HEAD_DIM)
            k_rows[:, lanes] = turn(qk_raw[:, k_lanes], k_scale, kg_ref, h)
        if step == 0:
            landing(k_copy, ctx_k.at[pl.ds(0, LAGS)]).wait_recv()
        for s in range(TEAM):
            span = slice(s * rows, (s + 1) * rows)
            for h in range(heads):
                lanes = slice(h * HEAD_DIM, (h + 1) * HEAD_DIM)
                query = q_rows[span, lanes]
                keys = ctx_k[s : s + LAGS, :, lanes].reshape(LAGS * rows, HEAD_DIM)
                values = ctx_v[s : s + LAGS, :, lanes].reshape(LAGS * rows, HEAD_DIM)
                own_values = buffer[
                    0, s, :, pl.ds(pl.multiple_of(rank * inner + h * HEAD_DIM, 128), HEAD_DIM)
                ]
                near = lax.dot_general(
                    query, k_rows[span, lanes], nt, preferred_element_type=jnp.float32
                ) * HEAD_DIM ** (-0.5)
                past = lax.dot_general(
                    query, keys, nt, preferred_element_type=jnp.float32
                ) * HEAD_DIM ** (-0.5) + bias_all[s, 0:1, :]
                highest = jnp.maximum(
                    jnp.max(near, axis=-1, keepdims=True), jnp.max(past, axis=-1, keepdims=True)
                )
                near = jnp.exp(near - highest)
                past = jnp.exp(past - highest)
                inverse = 1.0 / (
                    jnp.sum(near, axis=-1, keepdims=True) + jnp.sum(past, axis=-1, keepdims=True)
                )
                mixed = jnp.dot(
                    (near * inverse).astype(jnp.bfloat16), own_values,
                    preferred_element_type=jnp.float32,
                ) + jnp.dot(
                    (past * inverse).astype(jnp.bfloat16), values,
                    preferred_element_type=jnp.float32,
                )
                mix_out[step, s, :, lanes] = mixed.astype(jnp.bfloat16)
        waits = []
        for slot in (2, 3, 1):
            copy = remote(mix_out.at[step, ranks[slot]], mix.at[step, rank], peers[slot])
            go(copy)
            waits.append(landing(copy, mix.at[step, ranks[slot]]))
        mix[step, pl.ds(rank, 1)] = mix_out[step, pl.ds(rank, 1)]
        for wait in waits:
            wait.wait_recv()
        change = sig_ref[step]
        for r in range(TEAM):
            lanes = slice(r * inner, (r + 1) * inner)
            gate = mods[step + 1 : step + 2, 2 * width + r * inner : 2 * width + (r + 1) * inner]
            fresh = (
                latent[:, lanes] + (change * gate) * mix[step, r].astype(jnp.float32)
            ).astype(jnp.bfloat16)
            if step == STEPS - 1:
                out_ref[:, lanes] = fresh
            else:
                latent[:, lanes] = fresh.astype(jnp.float32)

    for copy in started:
        copy.wait_send()


def fused(noisy, clean, seg_ids, lag_mask, plan, w_query, w_key, time_proj, q_gain, k_gain):
    rows, width = noisy.shape
    inner = w_query.shape[1] // TEAM
    count = lax.axis_size("fsdp")
    me = lax.axis_index("fsdp")
    spans = (me // TEAM) * TEAM + jnp.arange(TEAM, dtype=jnp.int32)
    starts = jnp.sum((seg_ids[None, :] < seg_ids[spans][:, None]).astype(jnp.int32), axis=1)
    positions = (
        (spans - starts)[:, None] * rows + jnp.arange(rows, dtype=jnp.int32)[None, :]
    ).reshape(-1).astype(jnp.float32)
    half_count = HEAD_DIM // 2
    angles = positions[:, None] * frequencies(half_count)[None, :]
    cosine, sine = jnp.cos(angles), jnp.sin(angles)
    cosine = jnp.concatenate([cosine, cosine], axis=1)
    sine = jnp.concatenate([-sine, sine], axis=1)
    levels = sigma_of(plan[0])
    sigmas = jnp.concatenate([jnp.zeros((1,), jnp.float32), levels, jnp.zeros((5,), jnp.float32)])
    turns = 1000.0 * sigmas[:, None] * frequencies(time_proj.shape[0] // 2)[None, :]
    features = jnp.concatenate([jnp.cos(turns), jnp.sin(turns)], axis=1).astype(jnp.bfloat16)
    changes = jnp.concatenate([levels[1:], jnp.zeros((1,), jnp.float32)]) - levels
    pieces = []
    for distance in range(LAGS, 0, -1):
        source = jnp.maximum(me - distance, 0)
        allowed = (
            (me >= distance)
            & (seg_ids[source] == seg_ids[me])
            & (lag_mask[0, distance - 1] == 1)
        )
        pieces.append(jnp.full((rows,), jnp.where(allowed, 0.0, MASKED), jnp.float32))
    bias = jnp.broadcast_to(jnp.concatenate(pieces)[None, :], (8, LAGS * rows))
    vmem = pl.BlockSpec(memory_space=pltpu.VMEM)
    total = TEAM * rows
    bf16, f32 = jnp.bfloat16, jnp.float32
    copies = 96 + 4 * count
    return pl.pallas_call(
        functools.partial(fused_kernel, count),
        out_shape=jax.ShapeDtypeStruct(noisy.shape, bf16),
        in_specs=[vmem, vmem, pl.BlockSpec(memory_space=pltpu.SMEM)] + [vmem] * 9,
        out_specs=vmem,
        scratch_shapes=[
            pltpu.VMEM((width, 2 * inner), bf16),
            pltpu.VMEM((2, TEAM, rows, width), bf16),
            pltpu.VMEM((1, TEAM, rows, width), bf16),
            pltpu.VMEM((LAGS + TEAM, rows, inner), bf16),
            pltpu.VMEM((LAGS + TEAM, rows, inner), bf16),
            pltpu.VMEM((total, 2 * inner), f32),
            pltpu.VMEM((total, inner), f32),
            pltpu.VMEM((STEPS, TEAM, 8, total), f32),
            pltpu.VMEM((STEPS, TEAM, rows, inner), bf16),
            pltpu.VMEM((STEPS, TEAM, rows, inner), bf16),
            pltpu.VMEM((rows, width), f32),
            pltpu.VMEM((8, 3 * width), f32),
            pltpu.VMEM((total, inner), bf16),
            pltpu.VMEM((total, inner), bf16),
            pltpu.VMEM((TEAM, 8, LAGS * rows), f32),
            pltpu.SemaphoreType.DMA((copies,)),
            pltpu.SemaphoreType.DMA((copies,)),
            pltpu.SemaphoreType.DMA((2,)),
        ],
        compiler_params=pltpu.CompilerParams(
            collective_id=0, has_side_effects=True, vmem_limit_bytes=48 * 1024 * 1024
        ),
    )(
        bias, features, changes, cosine, sine, noisy, clean, w_query, w_key, time_proj,
        q_gain[None, :], k_gain[None, :],
    )


def body(*arrays):
    part = arrays[5].shape[0]
    aligned = lax.axis_size("fsdp") % (2 * TEAM) == 0 and part % 16 == 0
    return (fused if aligned else local)(*arrays)


def solution(mesh):
    placed = (
        P(("pool", "fsdp"), None),
        P(("pool", "fsdp"), None),
        P("pool"),
        P(("pool", "fsdp"), None),
        P(("pool", "fsdp"), None),
        P("fsdp", None),
        P("fsdp", None),
        P(),
        P(),
        P(),
    )
    return jax.shard_map(
        body, mesh=mesh, in_specs=placed, out_specs=P(("pool", "fsdp"), None), check_vma=False
    )
```

```python
import functools
import math

import jax
import jax.numpy as jnp
from jax import lax
from jax.experimental import pallas as pl
from jax.experimental.pallas import tpu as pltpu
from jax.sharding import PartitionSpec as P

HEADS = 20
HEAD_DIM = 128
STEPS = 2
LAGS = 2
LEVELS = 1000


SIGMA_SHIFT = 5.0
EPSILON = 1e-06
MASKED = -1e30


def passed_along(value, axis, steps):
    count = lax.axis_size(axis)
    leading, last = (max(0, -steps), min(count, count - steps))
    return lax.ppermute(value, axis, [(source, source + steps) for source in range(leading, last)])


def sigma_of(levels):
    fraction = levels.astype(jnp.float32) / LEVELS
    return SIGMA_SHIFT * fraction / (1.0 + (SIGMA_SHIFT - 1.0) * fraction)


def frequencies(half_count):
    return jnp.exp(-math.log(10000.0) * jnp.arange(half_count, dtype=jnp.float32) / half_count)


def modulation(sigmas, time_proj):
    half_count = time_proj.shape[0] // 2
    angles = 1000.0 * sigmas[:, None] * frequencies(half_count)[None, :]
    features = jnp.concatenate([jnp.cos(angles), jnp.sin(angles)], axis=1).astype(jnp.bfloat16)
    return jnp.dot(features, time_proj, preferred_element_type=jnp.float32)[0]


def modulate(latent, mod_row, model_width):
    values = latent.astype(jnp.float32)
    centred = values - jnp.mean(values, axis=-1, keepdims=True)
    variance = jnp.mean(centred * centred, axis=-1, keepdims=True)
    normed = centred * lax.rsqrt(variance + EPSILON)
    return (normed * (1.0 + mod_row[model_width : 2 * model_width]) + mod_row[:model_width]).astype(
        jnp.bfloat16
    )


def normalize(values, gain):
    mean_square = jnp.mean(values * values, axis=-1, keepdims=True)
    return values * lax.rsqrt(mean_square + EPSILON) * gain


def rotate(values, positions):
    half_count = HEAD_DIM // 2
    split_heads = values.reshape(values.shape[:-1] + (HEADS, HEAD_DIM))
    angles = positions[..., None] * frequencies(half_count)
    cosine = jnp.cos(angles)[..., None, :]
    sine = jnp.sin(angles)[..., None, :]
    front = split_heads[..., :half_count]
    back = split_heads[..., half_count:]
    turned = jnp.concatenate([front * cosine - back * sine, front * sine + back * cosine], axis=-1)
    return turned.reshape(values.shape)


def attend(query_rows, key_rows, value_rows, usable):
    row_count = query_rows.shape[0]
    query_heads = query_rows.reshape(row_count, HEADS, HEAD_DIM)
    key_heads = key_rows.reshape(-1, HEADS, HEAD_DIM)
    value_heads = value_rows.reshape(-1, HEADS, HEAD_DIM)
    scores = jnp.einsum(
        "qhd,khd->hqk", query_heads, key_heads, preferred_element_type=jnp.float32
    ) * HEAD_DIM ** (-0.5)
    scores = jnp.where(usable[None, None, :], scores, MASKED)
    highest = jnp.max(scores, axis=-1, keepdims=True)
    expanded = jnp.exp(scores - highest)
    weights = (expanded / jnp.sum(expanded, axis=-1, keepdims=True)).astype(jnp.bfloat16)
    mixed = jnp.einsum("hqk,khd->qhd", weights, value_heads, preferred_element_type=jnp.float32)
    return mixed.reshape(row_count, HEADS * HEAD_DIM).astype(jnp.bfloat16)


def make_absorbers(noisy_hidden, context_hidden):

    def absorb_both(carry, pieces, offset):
        stored = tuple((piece_rows for piece_rows in pieces))
        query_sum = jnp.dot(noisy_hidden, pieces[0], preferred_element_type=jnp.float32)
        key_sum = jnp.dot(noisy_hidden, pieces[1], preferred_element_type=jnp.float32)
        ctxkey_sum = jnp.dot(context_hidden, pieces[1], preferred_element_type=jnp.float32)
        return (stored, (query_sum, key_sum, ctxkey_sum))

    def absorb_key(carry, piece, offset):
        buffer_rows, partials = carry
        stored = lax.dynamic_update_slice_in_dim(buffer_rows, piece, offset, 0)
        key_sum, ctxkey_sum = partials
        key_sum = key_sum + jnp.dot(noisy_hidden, piece, preferred_element_type=jnp.float32)
        ctxkey_sum = ctxkey_sum + jnp.dot(context_hidden, piece, preferred_element_type=jnp.float32)
        return (stored, (key_sum, ctxkey_sum))

    def absorb_query(carry, piece, offset):
        buffer_rows, query_sum = carry
        stored = lax.dynamic_update_slice_in_dim(buffer_rows, piece, offset, 0)
        query_sum = query_sum + jnp.dot(noisy_hidden, piece, preferred_element_type=jnp.float32)
        return (stored, query_sum)

    return (absorb_both, absorb_key, absorb_query)


def local(noisy, clean, seg_ids, lag_mask, plan, w_query, w_key, time_proj, q_gain, k_gain):
    row_count, model_width = noisy.shape
    inner_width = w_query.shape[1]
    span_index = lax.axis_index("fsdp")
    segment_start = jnp.sum((seg_ids < seg_ids[span_index]).astype(jnp.int32))
    span_place = span_index - segment_start
    positions = (span_place * row_count + jnp.arange(row_count, dtype=jnp.int32)).astype(
        jnp.float32
    )
    sigmas = [sigma_of(plan[0, level_index : level_index + 1]) for level_index in range(STEPS)] + [
        jnp.zeros((1,), jnp.float32)
    ]
    rest_mod = modulation(jnp.zeros((1,), jnp.float32), time_proj)
    step_mods = [modulation(sigmas[level_index], time_proj) for level_index in range(STEPS)]
    context_hidden = modulate(clean, rest_mod, model_width)
    noisy_hidden = modulate(noisy, step_mods[0], model_width)
    absorb_both, absorb_key, absorb_query = make_absorbers(noisy_hidden, context_hidden)
    empty_buffer = jnp.zeros((model_width, inner_width), jnp.bfloat16)
    empty_sum = jnp.zeros((row_count, inner_width), jnp.float32)
    buffers, partials = absorb_both(
        ((empty_buffer, empty_buffer), (empty_sum, empty_sum, empty_sum)),
        (
            lax.all_gather(w_query, "fsdp", axis=0, tiled=True),
            lax.all_gather(w_key, "fsdp", axis=0, tiled=True),
        ),
        jnp.int32(0),
    )
    full_query, full_key = buffers
    query_sum, key_sum, ctxkey_sum = partials
    context_key = rotate(normalize(ctxkey_sum, k_gain), positions).astype(jnp.bfloat16)
    context_pair = jnp.stack([context_key, context_hidden])
    received = [passed_along(context_pair, "fsdp", 1)]
    distance = 2
    received.append(passed_along(context_pair, "fsdp", distance))
    usable_parts = [jnp.ones((row_count,), jnp.int32) > 0]
    for distance in range(1, LAGS + 1):
        source = jnp.maximum(span_index - distance, 0)
        allowed = (
            (span_index >= distance)
            & (seg_ids[source] == seg_ids[span_index])
            & (lag_mask[0, distance - 1] == 1)
        )
        usable_parts.append(jnp.broadcast_to(allowed, (row_count,)))
    usable = jnp.concatenate(usable_parts)
    keys_context = jnp.concatenate([pair_rows[0] for pair_rows in received], axis=0)
    values_context = jnp.concatenate([pair_rows[1] for pair_rows in received], axis=0)
    latent = noisy
    for step_index in range(STEPS):
        if step_index == 0:
            hidden = noisy_hidden
            query_raw, key_raw = (query_sum, key_sum)
        else:
            hidden = modulate(latent, step_mods[step_index], model_width)
            query_raw = jnp.dot(hidden, full_query, preferred_element_type=jnp.float32)
            key_raw = jnp.dot(hidden, full_key, preferred_element_type=jnp.float32)
        query_rows = rotate(normalize(query_raw, q_gain), positions).astype(jnp.bfloat16)
        key_rows = rotate(normalize(key_raw, k_gain), positions).astype(jnp.bfloat16)
        mixed = attend(
            query_rows,
            jnp.concatenate([key_rows, keys_context], axis=0),
            jnp.concatenate([hidden, values_context], axis=0),
            usable,
        )
        sigma_change = sigmas[step_index + 1] - sigmas[step_index]
        factor = sigma_change * step_mods[step_index][2 * model_width :]
        latent = (latent.astype(jnp.float32) + factor[None, :] * mixed.astype(jnp.float32)).astype(
            jnp.bfloat16
        )
    return latent


TEAM = 4
MESH = pl.DeviceIdType.MESH


def fused_kernel(
    count, seg_ref, lag_ref, plan_ref, noisy_ref, clean_ref, wq_ref, wk_ref, proj_ref, qg_ref,
    kg_ref, out_ref,
    w_all, hid, hid2, ctx_k, ctx_v, qk_raw, ck_raw, stat, mix, mix_out, latent, mods, q_rows, k_rows,
    bias_all, cos_ref, sin_ref, send_sem, recv_sem, local_sem,
):
    rows, width = noisy_ref.shape
    part = wq_ref.shape[0]
    inner = wq_ref.shape[1] // TEAM
    heads = inner // HEAD_DIM
    groups = count // TEAM
    half = groups // 2
    me = lax.axis_index("fsdp")
    group = me // TEAM
    rank = me % TEAM
    sib_rank = rank + 1 - 2 * (rank % 2)
    far_rank = (rank + 2) % TEAM
    diag_rank = (sib_rank + 2) % TEAM
    ranks = [rank, sib_rank, far_rank, diag_rank]
    low = group % 2
    spot = group // 2 + low * (groups - 1 - 2 * (group // 2))

    def group_at(place):
        place = (place + 2 * groups) % groups
        upper = place // half
        return 2 * (place + upper * (groups - 1 - 2 * place)) + upper

    base = group * TEAM
    peers = [base + r for r in ranks]
    ring_next = group_at(spot + 1) * TEAM + rank
    ring_prev = group_at(spot - 1) * TEAM + rank
    later = ((group + 1) % groups) * TEAM + rank
    earlier = ((group + groups - 1) % groups) * TEAM + rank

    def cols(r):
        return pl.ds(pl.multiple_of(r * inner, 128), inner)

    def wrows(device):
        return pl.ds(pl.multiple_of(device * part, 16), part)

    barrier = pltpu.get_barrier_semaphore()
    friends = peers[1:] + [ring_next, ring_prev, later, earlier]
    for friend in friends:
        pl.semaphore_signal(barrier, inc=1, device_id={"fsdp": friend}, device_id_type=MESH)

    own = [
        pltpu.make_async_copy(
            ref.at[:, cols(rank)], w_all.at[wrows(me), pl.ds(k * inner, inner)], local_sem.at[k]
        )
        for k, ref in enumerate((wq_ref, wk_ref))
    ]
    for copy in own:
        copy.start()
    for copy in own:
        copy.wait()
    pl.semaphore_wait(barrier, len(friends))

    used = [0]
    started = []

    def remote(src, dst, target):
        index = used[0]
        used[0] += 1
        copy = pltpu.make_async_remote_copy(
            src_ref=src, dst_ref=dst, send_sem=send_sem.at[index], recv_sem=recv_sem.at[index],
            device_id={"fsdp": target}, device_id_type=MESH,
        )
        return copy, index

    def go(copy):
        copy[0].start()
        started.append(copy[0])

    def landing(copy, dst):
        return pltpu.make_async_remote_copy(
            src_ref=dst, dst_ref=dst, send_sem=send_sem.at[copy[1]],
            recv_sem=recv_sem.at[copy[1]], device_id={"fsdp": peers[1]}, device_id_type=MESH,
        )

    def ring_send(step, slot):
        arrivals = []
        for sign, target in ((1, ring_next), (-1, ring_prev)):
            lanes = pl.ds(0, 2 * inner)
            if step == half - 1:
                lanes = pl.ds(0, inner) if sign == 1 else pl.ds(inner, inner)
            source = group_at(spot - sign * step) * TEAM + ranks[slot]
            view = w_all.at[wrows(source), lanes]
            copy = remote(view, view, target)
            go(copy)
            coming = group_at(spot - sign * (step + 1)) * TEAM + ranks[slot]
            arrivals.append((copy, w_all.at[wrows(coming), lanes]))
        return arrivals

    ring = {}
    ring[0, 0] = ring_send(0, 0)
    scatter = {}
    for slot in range(1, TEAM):
        for k, ref in enumerate((wq_ref, wk_ref)):
            lanes = pl.ds(k * inner, inner)
            copy = remote(ref.at[:, cols(ranks[slot])], w_all.at[wrows(me), lanes], peers[slot])
            go(copy)
            scatter[slot, k] = (copy, w_all.at[wrows(peers[slot]), lanes])

    def lane_frequencies(shape, half_count):
        lane = lax.broadcasted_iota(jnp.int32, shape, 1) % half_count
        return jnp.exp(lane.astype(jnp.float32) * (-math.log(10000.0) / half_count))

    def sigma_rows(step):
        level = jnp.full((8, proj_ref.shape[0]), plan_ref[0, step], jnp.int32)
        return sigma_of(level)

    steps_sigma = [sigma_rows(step) for step in range(STEPS)]
    row_at = lax.broadcasted_iota(jnp.int32, steps_sigma[0].shape, 0)
    sigmas = jnp.zeros(steps_sigma[0].shape, jnp.float32)
    for step in range(STEPS):
        sigmas = jnp.where(row_at == step + 1, steps_sigma[step], sigmas)
    time_half = proj_ref.shape[0] // 2
    turns = 1000.0 * sigmas * lane_frequencies(sigmas.shape, time_half)
    first = lax.broadcasted_iota(jnp.int32, sigmas.shape, 1) < time_half
    features = jnp.where(first, jnp.cos(turns), jnp.sin(turns)).astype(jnp.bfloat16)
    mods[...] = jnp.dot(features, proj_ref[...], preferred_element_type=jnp.float32)

    def modulated(values, index):
        centred = values - jnp.mean(values, axis=-1, keepdims=True)
        variance = jnp.mean(centred * centred, axis=-1, keepdims=True)
        normed = centred * lax.rsqrt(variance + EPSILON)
        scale = mods[index : index + 1, width : 2 * width]
        return (normed * (1.0 + scale) + mods[index : index + 1, :width]).astype(jnp.bfloat16)

    def share(buffer, lead):
        own_view = buffer.at[lead + (rank,)]
        to_sib = remote(own_view, own_view, peers[1])
        to_far = remote(own_view, own_view, peers[2])
        go(to_far)
        go(to_sib)
        return (
            landing(to_sib, buffer.at[lead + (sib_rank,)]),
            landing(to_far, buffer.at[lead + (far_rank,)]),
        )

    def share_rest(buffer, lead, pending):
        from_sib, from_far = pending
        from_far.wait_recv()
        view = buffer.at[lead + (far_rank,)]
        forward = remote(view, view, peers[1])
        go(forward)
        from_sib.wait_recv()
        landing(forward, buffer.at[lead + (diag_rank,)]).wait_recv()

    def share_all(buffer, lead):
        waits = []
        view = buffer.at[lead + (rank,)]
        for slot in (2, 3, 1):
            copy = remote(view, view, peers[slot])
            go(copy)
            waits.append(landing(copy, buffer.at[lead + (ranks[slot],)]))
        return waits

    def pass_own(slot):
        for k in range(2):
            copy, view = scatter[slot, k]
            landing(copy, view).wait_recv()
        ring[0, slot] = ring_send(0, slot)

    def pass_on(step, slot):
        if step < half:
            for copy, view in ring[step - 1, slot]:
                landing(copy, view).wait_recv()
            ring[step, slot] = ring_send(step, slot)

    pass_own(1)
    latent[...] = noisy_ref[...].astype(jnp.float32)
    hid[0, pl.ds(rank, 1)] = modulated(latent[...], 1)[None]
    pending_noisy = share(hid, (0,))
    pass_on(1, 0)
    pass_own(2)
    pass_own(3)
    hid[1, pl.ds(rank, 1)] = modulated(clean_ref[...].astype(jnp.float32), 0)[None]
    pending_clean = share(hid, (1,))
    here = seg_ref[me]
    bias_lane = lax.broadcasted_iota(jnp.int32, (8, LAGS * rows), 1) // rows
    bias = jnp.zeros((8, LAGS * rows), jnp.float32)
    for distance in range(1, LAGS + 1):
        source = jnp.maximum(me - distance, 0)
        level = jnp.where(seg_ref[source] == here, 0.0, MASKED)
        level = jnp.where(lag_ref[0, distance - 1] == 1, level, MASKED)
        level = jnp.where(me >= distance, level, MASKED)
        bias = jnp.where(bias_lane == LAGS - distance, level, bias)
    bias_all[pl.ds(rank, 1)] = bias[None]
    pending_bias = share_all(bias_all, ())
    pass_on(1, 1)
    pass_on(1, 2)
    share_rest(hid, (0,), pending_noisy)
    pass_on(1, 3)
    share_rest(hid, (1,), pending_clean)
    pass_on(2, 0)
    for wait in pending_bias:
        wait.wait_recv()

    for s in range(TEAM):
        ctx_v[LAGS + s] = hid[1, s, :, cols(rank)]
    v_copy = remote(ctx_v.at[pl.ds(TEAM, LAGS)], ctx_v.at[pl.ds(0, LAGS)], later)
    go(v_copy)
    for slot in range(1, TEAM):
        pass_on(2, slot)

    half_count = HEAD_DIM // 2
    for s in range(TEAM):
        span_id = seg_ref[base + s]
        start = jnp.int32(0)
        for other in range(count):
            start = start + jnp.where(seg_ref[other] < span_id, 1, 0)
        place = (base + s - start) * rows
        shape = (rows, HEAD_DIM)
        position = (lax.broadcasted_iota(jnp.int32, shape, 0) + place).astype(jnp.float32)
        angles = position * lane_frequencies(shape, half_count)
        sine = jnp.sin(angles)
        front = lax.broadcasted_iota(jnp.int32, shape, 1) < half_count
        cos_ref[s * rows : (s + 1) * rows] = jnp.cos(angles)
        sin_ref[s * rows : (s + 1) * rows] = jnp.where(front, -sine, sine)

    for step in range(3, half):
        for slot in range(TEAM):
            pass_on(step, slot)
    for slot in range(TEAM):
        for copy, view in ring[half - 1, slot]:
            landing(copy, view).wait_recv()
    landing(v_copy, ctx_v.at[pl.ds(0, LAGS)]).wait_recv()

    all_rows = TEAM * rows

    def project(source, first, last, target):
        start = first
        while start < last:
            size = min(256, last - start)
            target[:, start - first : start - first + size] = jnp.dot(
                source, w_all[:, start : start + size], preferred_element_type=jnp.float32
            )
            start += size

    ones = jnp.ones((8, inner), jnp.float32)
    nt = (((1,), (1,)), ((), ()))

    def squares(values):
        return lax.dot_general(
            ones, values * values, nt, precision=lax.Precision.HIGHEST,
            preferred_element_type=jnp.float32,
        )

    def row_scale(sums, index):
        pick = (lax.broadcasted_iota(jnp.int32, (8, 128), 0) == index).astype(jnp.float32)
        total = lax.dot_general(
            sums, pick, (((0,), (0,)), ((), ())), precision=lax.Precision.HIGHEST,
            preferred_element_type=jnp.float32,
        )
        return lax.rsqrt(total * (1.0 / width) + EPSILON)

    def turn(values, scale, gain_ref, h):
        gain = gain_ref[pl.ds(pl.multiple_of(rank * inner + h * HEAD_DIM, 128), HEAD_DIM)]
        value = values * scale * gain[None, :]
        rolled = pltpu.roll(value, HEAD_DIM // 2, 1)
        return (value * cos_ref[...] + rolled * sin_ref[...]).astype(jnp.bfloat16)

    for step in range(STEPS):
        buffer = hid if step == 0 else hid2
        if step == 1:
            hid2[0, pl.ds(rank, 1)] = modulated(latent[...], 2)[None]
            share_rest(hid2, (0,), share(hid2, (0,)))
        rows_in = buffer[0].reshape(all_rows, width)
        project(rows_in, 0, 2 * inner, qk_raw)
        if step == 0:
            project(hid[1].reshape(all_rows, width), inner, 2 * inner, ck_raw)
        row_kind = lax.broadcasted_iota(jnp.int32, (8, all_rows), 0)
        sums = jnp.where(
            row_kind == 0, squares(qk_raw[:, :inner]), squares(qk_raw[:, inner:])
        )
        if step == 0:
            sums = jnp.where(row_kind == 2, squares(ck_raw[...]), sums)
        stat[step, pl.ds(rank, 1)] = sums[None]
        for wait in share_all(stat, (step,)):
            wait.wait_recv()
        total = stat[step, 0] + stat[step, 1] + stat[step, 2] + stat[step, 3]
        if step == 0:
            c_scale = row_scale(total, 2)
            for h in range(heads):
                lanes = slice(h * HEAD_DIM, (h + 1) * HEAD_DIM)
                turned = turn(ck_raw[:, lanes], c_scale, kg_ref, h)
                ctx_k[LAGS : LAGS + TEAM, :, lanes] = turned.reshape(TEAM, rows, HEAD_DIM)
            k_copy = remote(ctx_k.at[pl.ds(TEAM, LAGS)], ctx_k.at[pl.ds(0, LAGS)], later)
            go(k_copy)
        q_scale = row_scale(total, 0)
        k_scale = row_scale(total, 1)
        for h in range(heads):
            lanes = slice(h * HEAD_DIM, (h + 1) * HEAD_DIM)
            q_rows[:, lanes] = turn(qk_raw[:, lanes], q_scale, qg_ref, h)
            k_lanes = slice(inner + h * HEAD_DIM, inner + (h + 1) * HEAD_DIM)
            k_rows[:, lanes] = turn(qk_raw[:, k_lanes], k_scale, kg_ref, h)
        if step == 0:
            landing(k_copy, ctx_k.at[pl.ds(0, LAGS)]).wait_recv()
        for s in range(TEAM):
            span = slice(s * rows, (s + 1) * rows)
            for h in range(heads):
                lanes = slice(h * HEAD_DIM, (h + 1) * HEAD_DIM)
                query = q_rows[span, lanes]
                keys = ctx_k[s : s + LAGS, :, lanes].reshape(LAGS * rows, HEAD_DIM)
                values = ctx_v[s : s + LAGS, :, lanes].reshape(LAGS * rows, HEAD_DIM)
                own_values = buffer[
                    0, s, :, pl.ds(pl.multiple_of(rank * inner + h * HEAD_DIM, 128), HEAD_DIM)
                ]
                near = lax.dot_general(
                    query, k_rows[span, lanes], nt, preferred_element_type=jnp.float32
                ) * HEAD_DIM ** (-0.5)
                past = lax.dot_general(
                    query, keys, nt, preferred_element_type=jnp.float32
                ) * HEAD_DIM ** (-0.5) + bias_all[s, 0:1, :]
                highest = jnp.maximum(
                    jnp.max(near, axis=-1, keepdims=True), jnp.max(past, axis=-1, keepdims=True)
                )
                near = jnp.exp(near - highest)
                past = jnp.exp(past - highest)
                inverse = 1.0 / (
                    jnp.sum(near, axis=-1, keepdims=True) + jnp.sum(past, axis=-1, keepdims=True)
                )
                mixed = jnp.dot(
                    (near * inverse).astype(jnp.bfloat16), own_values,
                    preferred_element_type=jnp.float32,
                ) + jnp.dot(
                    (past * inverse).astype(jnp.bfloat16), values,
                    preferred_element_type=jnp.float32,
                )
                mix_out[step, s, :, lanes] = mixed.astype(jnp.bfloat16)
        waits = []
        for slot in (2, 3, 1):
            copy = remote(mix_out.at[step, ranks[slot]], mix.at[step, rank], peers[slot])
            go(copy)
            waits.append(landing(copy, mix.at[step, ranks[slot]]))
        mix[step, pl.ds(rank, 1)] = mix_out[step, pl.ds(rank, 1)]
        for wait in waits:
            wait.wait_recv()
        change = -steps_sigma[step][:1, :1]
        if step + 1 < STEPS:
            change = change + steps_sigma[step + 1][:1, :1]
        for r in range(TEAM):
            lanes = slice(r * inner, (r + 1) * inner)
            gate = mods[step + 1 : step + 2, 2 * width + r * inner : 2 * width + (r + 1) * inner]
            fresh = (
                latent[:, lanes] + (change * gate) * mix[step, r].astype(jnp.float32)
            ).astype(jnp.bfloat16)
            if step == STEPS - 1:
                out_ref[:, lanes] = fresh
            else:
                latent[:, lanes] = fresh.astype(jnp.float32)

    for copy in started:
        copy.wait_send()


def fused(noisy, clean, seg_ids, lag_mask, plan, w_query, w_key, time_proj, q_gain, k_gain):
    rows, width = noisy.shape
    inner = w_query.shape[1] // TEAM
    count = lax.axis_size("fsdp")
    vmem = pl.BlockSpec(memory_space=pltpu.VMEM)
    total = TEAM * rows
    bf16, f32 = jnp.bfloat16, jnp.float32
    copies = 96 + 4 * count
    return pl.pallas_call(
        functools.partial(fused_kernel, count),
        out_shape=jax.ShapeDtypeStruct(noisy.shape, bf16),
        in_specs=[pl.BlockSpec(memory_space=pltpu.SMEM)] * 3 + [vmem] * 7,
        out_specs=vmem,
        scratch_shapes=[
            pltpu.VMEM((width, 2 * inner), bf16),
            pltpu.VMEM((2, TEAM, rows, width), bf16),
            pltpu.VMEM((1, TEAM, rows, width), bf16),
            pltpu.VMEM((LAGS + TEAM, rows, inner), bf16),
            pltpu.VMEM((LAGS + TEAM, rows, inner), bf16),
            pltpu.VMEM((total, 2 * inner), f32),
            pltpu.VMEM((total, inner), f32),
            pltpu.VMEM((STEPS, TEAM, 8, total), f32),
            pltpu.VMEM((STEPS, TEAM, rows, inner), bf16),
            pltpu.VMEM((STEPS, TEAM, rows, inner), bf16),
            pltpu.VMEM((rows, width), f32),
            pltpu.VMEM((8, 3 * width), f32),
            pltpu.VMEM((total, inner), bf16),
            pltpu.VMEM((total, inner), bf16),
            pltpu.VMEM((TEAM, 8, LAGS * rows), f32),
            pltpu.VMEM((total, HEAD_DIM), f32),
            pltpu.VMEM((total, HEAD_DIM), f32),
            pltpu.SemaphoreType.DMA((copies,)),
            pltpu.SemaphoreType.DMA((copies,)),
            pltpu.SemaphoreType.DMA((2,)),
        ],
        compiler_params=pltpu.CompilerParams(
            collective_id=0, has_side_effects=True, vmem_limit_bytes=48 * 1024 * 1024
        ),
    )(
        seg_ids, lag_mask, plan, noisy, clean, w_query, w_key, time_proj, q_gain, k_gain,
    )


def body(*arrays):
    part = arrays[5].shape[0]
    aligned = lax.axis_size("fsdp") % (2 * TEAM) == 0 and part % 16 == 0
    return (fused if aligned else local)(*arrays)


def solution(mesh):
    placed = (
        P(("pool", "fsdp"), None),
        P(("pool", "fsdp"), None),
        P("pool"),
        P(("pool", "fsdp"), None),
        P(("pool", "fsdp"), None),
        P("fsdp", None),
        P("fsdp", None),
        P(),
        P(),
        P(),
    )
    return jax.shard_map(
        body, mesh=mesh, in_specs=placed, out_specs=P(("pool", "fsdp"), None), check_vma=False
    )
```

```python
import functools
import math

import jax
import jax.numpy as jnp
from jax import lax
from jax.experimental import pallas as pl
from jax.experimental.pallas import tpu as pltpu
from jax.sharding import PartitionSpec as P

HEADS = 20
HEAD_DIM = 128
STEPS = 2
LAGS = 2
LEVELS = 1000


SIGMA_SHIFT = 5.0
EPSILON = 1e-06
MASKED = -1e30


def passed_along(value, axis, steps):
    count = lax.axis_size(axis)
    leading, last = (max(0, -steps), min(count, count - steps))
    return lax.ppermute(value, axis, [(source, source + steps) for source in range(leading, last)])


def sigma_of(levels):
    fraction = levels.astype(jnp.float32) / LEVELS
    return SIGMA_SHIFT * fraction / (1.0 + (SIGMA_SHIFT - 1.0) * fraction)


def frequencies(half_count):
    return jnp.exp(-math.log(10000.0) * jnp.arange(half_count, dtype=jnp.float32) / half_count)


def modulation(sigmas, time_proj):
    half_count = time_proj.shape[0] // 2
    angles = 1000.0 * sigmas[:, None] * frequencies(half_count)[None, :]
    features = jnp.concatenate([jnp.cos(angles), jnp.sin(angles)], axis=1).astype(jnp.bfloat16)
    return jnp.dot(features, time_proj, preferred_element_type=jnp.float32)[0]


def modulate(latent, mod_row, model_width):
    values = latent.astype(jnp.float32)
    centred = values - jnp.mean(values, axis=-1, keepdims=True)
    variance = jnp.mean(centred * centred, axis=-1, keepdims=True)
    normed = centred * lax.rsqrt(variance + EPSILON)
    return (normed * (1.0 + mod_row[model_width : 2 * model_width]) + mod_row[:model_width]).astype(
        jnp.bfloat16
    )


def normalize(values, gain):
    mean_square = jnp.mean(values * values, axis=-1, keepdims=True)
    return values * lax.rsqrt(mean_square + EPSILON) * gain


def rotate(values, positions):
    half_count = HEAD_DIM // 2
    split_heads = values.reshape(values.shape[:-1] + (HEADS, HEAD_DIM))
    angles = positions[..., None] * frequencies(half_count)
    cosine = jnp.cos(angles)[..., None, :]
    sine = jnp.sin(angles)[..., None, :]
    front = split_heads[..., :half_count]
    back = split_heads[..., half_count:]
    turned = jnp.concatenate([front * cosine - back * sine, front * sine + back * cosine], axis=-1)
    return turned.reshape(values.shape)


def attend(query_rows, key_rows, value_rows, usable):
    row_count = query_rows.shape[0]
    query_heads = query_rows.reshape(row_count, HEADS, HEAD_DIM)
    key_heads = key_rows.reshape(-1, HEADS, HEAD_DIM)
    value_heads = value_rows.reshape(-1, HEADS, HEAD_DIM)
    scores = jnp.einsum(
        "qhd,khd->hqk", query_heads, key_heads, preferred_element_type=jnp.float32
    ) * HEAD_DIM ** (-0.5)
    scores = jnp.where(usable[None, None, :], scores, MASKED)
    highest = jnp.max(scores, axis=-1, keepdims=True)
    expanded = jnp.exp(scores - highest)
    weights = (expanded / jnp.sum(expanded, axis=-1, keepdims=True)).astype(jnp.bfloat16)
    mixed = jnp.einsum("hqk,khd->qhd", weights, value_heads, preferred_element_type=jnp.float32)
    return mixed.reshape(row_count, HEADS * HEAD_DIM).astype(jnp.bfloat16)


def make_absorbers(noisy_hidden, context_hidden):

    def absorb_both(carry, pieces, offset):
        stored = tuple((piece_rows for piece_rows in pieces))
        query_sum = jnp.dot(noisy_hidden, pieces[0], preferred_element_type=jnp.float32)
        key_sum = jnp.dot(noisy_hidden, pieces[1], preferred_element_type=jnp.float32)
        ctxkey_sum = jnp.dot(context_hidden, pieces[1], preferred_element_type=jnp.float32)
        return (stored, (query_sum, key_sum, ctxkey_sum))

    def absorb_key(carry, piece, offset):
        buffer_rows, partials = carry
        stored = lax.dynamic_update_slice_in_dim(buffer_rows, piece, offset, 0)
        key_sum, ctxkey_sum = partials
        key_sum = key_sum + jnp.dot(noisy_hidden, piece, preferred_element_type=jnp.float32)
        ctxkey_sum = ctxkey_sum + jnp.dot(context_hidden, piece, preferred_element_type=jnp.float32)
        return (stored, (key_sum, ctxkey_sum))

    def absorb_query(carry, piece, offset):
        buffer_rows, query_sum = carry
        stored = lax.dynamic_update_slice_in_dim(buffer_rows, piece, offset, 0)
        query_sum = query_sum + jnp.dot(noisy_hidden, piece, preferred_element_type=jnp.float32)
        return (stored, query_sum)

    return (absorb_both, absorb_key, absorb_query)


def local(noisy, clean, seg_ids, lag_mask, plan, w_query, w_key, time_proj, q_gain, k_gain):
    row_count, model_width = noisy.shape
    inner_width = w_query.shape[1]
    span_index = lax.axis_index("fsdp")
    segment_start = jnp.sum((seg_ids < seg_ids[span_index]).astype(jnp.int32))
    span_place = span_index - segment_start
    positions = (span_place * row_count + jnp.arange(row_count, dtype=jnp.int32)).astype(
        jnp.float32
    )
    sigmas = [sigma_of(plan[0, level_index : level_index + 1]) for level_index in range(STEPS)] + [
        jnp.zeros((1,), jnp.float32)
    ]
    rest_mod = modulation(jnp.zeros((1,), jnp.float32), time_proj)
    step_mods = [modulation(sigmas[level_index], time_proj) for level_index in range(STEPS)]
    context_hidden = modulate(clean, rest_mod, model_width)
    noisy_hidden = modulate(noisy, step_mods[0], model_width)
    absorb_both, absorb_key, absorb_query = make_absorbers(noisy_hidden, context_hidden)
    empty_buffer = jnp.zeros((model_width, inner_width), jnp.bfloat16)
    empty_sum = jnp.zeros((row_count, inner_width), jnp.float32)
    buffers, partials = absorb_both(
        ((empty_buffer, empty_buffer), (empty_sum, empty_sum, empty_sum)),
        (
            lax.all_gather(w_query, "fsdp", axis=0, tiled=True),
            lax.all_gather(w_key, "fsdp", axis=0, tiled=True),
        ),
        jnp.int32(0),
    )
    full_query, full_key = buffers
    query_sum, key_sum, ctxkey_sum = partials
    context_key = rotate(normalize(ctxkey_sum, k_gain), positions).astype(jnp.bfloat16)
    context_pair = jnp.stack([context_key, context_hidden])
    received = [passed_along(context_pair, "fsdp", 1)]
    distance = 2
    received.append(passed_along(context_pair, "fsdp", distance))
    usable_parts = [jnp.ones((row_count,), jnp.int32) > 0]
    for distance in range(1, LAGS + 1):
        source = jnp.maximum(span_index - distance, 0)
        allowed = (
            (span_index >= distance)
            & (seg_ids[source] == seg_ids[span_index])
            & (lag_mask[0, distance - 1] == 1)
        )
        usable_parts.append(jnp.broadcast_to(allowed, (row_count,)))
    usable = jnp.concatenate(usable_parts)
    keys_context = jnp.concatenate([pair_rows[0] for pair_rows in received], axis=0)
    values_context = jnp.concatenate([pair_rows[1] for pair_rows in received], axis=0)
    latent = noisy
    for step_index in range(STEPS):
        if step_index == 0:
            hidden = noisy_hidden
            query_raw, key_raw = (query_sum, key_sum)
        else:
            hidden = modulate(latent, step_mods[step_index], model_width)
            query_raw = jnp.dot(hidden, full_query, preferred_element_type=jnp.float32)
            key_raw = jnp.dot(hidden, full_key, preferred_element_type=jnp.float32)
        query_rows = rotate(normalize(query_raw, q_gain), positions).astype(jnp.bfloat16)
        key_rows = rotate(normalize(key_raw, k_gain), positions).astype(jnp.bfloat16)
        mixed = attend(
            query_rows,
            jnp.concatenate([key_rows, keys_context], axis=0),
            jnp.concatenate([hidden, values_context], axis=0),
            usable,
        )
        sigma_change = sigmas[step_index + 1] - sigmas[step_index]
        factor = sigma_change * step_mods[step_index][2 * model_width :]
        latent = (latent.astype(jnp.float32) + factor[None, :] * mixed.astype(jnp.float32)).astype(
            jnp.bfloat16
        )
    return latent


TEAM = 4
MESH = pl.DeviceIdType.MESH


def fused_kernel(
    count, seg_ref, lag_ref, plan_ref, noisy_ref, clean_ref, wq_ref, wk_ref, proj_ref, qg_ref,
    kg_ref, out_ref,
    w_all, hid, hid2, ctx_k, ctx_v, qk_raw, ck_raw, stat, mix, mix_out, latent, mods, q_rows, k_rows,
    bias_all, cos_ref, sin_ref, send_sem, recv_sem, local_sem,
):
    rows, width = noisy_ref.shape
    part = wq_ref.shape[0]
    inner = wq_ref.shape[1] // TEAM
    heads = inner // HEAD_DIM
    groups = count // TEAM
    half = groups // 2
    me = lax.axis_index("fsdp")
    group = me // TEAM
    rank = me % TEAM
    sib_rank = rank + 1 - 2 * (rank % 2)
    far_rank = (rank + 2) % TEAM
    diag_rank = (sib_rank + 2) % TEAM
    ranks = [rank, sib_rank, far_rank, diag_rank]
    low = group % 2
    spot = group // 2 + low * (groups - 1 - 2 * (group // 2))

    def group_at(place):
        place = (place + 2 * groups) % groups
        upper = place // half
        return 2 * (place + upper * (groups - 1 - 2 * place)) + upper

    base = group * TEAM
    peers = [base + r for r in ranks]
    ring_next = group_at(spot + 1) * TEAM + rank
    ring_prev = group_at(spot - 1) * TEAM + rank
    later = ((group + 1) % groups) * TEAM + rank
    earlier = ((group + groups - 1) % groups) * TEAM + rank

    def cols(r):
        return pl.ds(pl.multiple_of(r * inner, 128), inner)

    def wrows(device):
        return pl.ds(pl.multiple_of(device * part, 16), part)

    barrier = pltpu.get_barrier_semaphore()
    friends = peers[1:] + [ring_next, ring_prev, later, earlier]
    for friend in friends:
        pl.semaphore_signal(barrier, inc=1, device_id={"fsdp": friend}, device_id_type=MESH)

    own = [
        pltpu.make_async_copy(
            ref.at[:, cols(rank)], w_all.at[wrows(me), pl.ds(k * inner, inner)], local_sem.at[k]
        )
        for k, ref in enumerate((wq_ref, wk_ref))
    ]
    for copy in own:
        copy.start()
    for copy in own:
        copy.wait()
    pl.semaphore_wait(barrier, len(friends))

    used = [0]
    started = []

    def remote(src, dst, target):
        index = used[0]
        used[0] += 1
        copy = pltpu.make_async_remote_copy(
            src_ref=src, dst_ref=dst, send_sem=send_sem.at[index], recv_sem=recv_sem.at[index],
            device_id={"fsdp": target}, device_id_type=MESH,
        )
        return copy, index

    def go(copy):
        copy[0].start()
        started.append(copy[0])

    def landing(copy, dst):
        return pltpu.make_async_remote_copy(
            src_ref=dst, dst_ref=dst, send_sem=send_sem.at[copy[1]],
            recv_sem=recv_sem.at[copy[1]], device_id={"fsdp": peers[1]}, device_id_type=MESH,
        )

    def ring_send(step, slot):
        arrivals = []
        for sign, target in ((1, ring_next), (-1, ring_prev)):
            lanes = pl.ds(0, 2 * inner)
            if step == half - 1:
                lanes = pl.ds(0, inner) if sign == 1 else pl.ds(inner, inner)
            source = group_at(spot - sign * step) * TEAM + ranks[slot]
            view = w_all.at[wrows(source), lanes]
            copy = remote(view, view, target)
            go(copy)
            coming = group_at(spot - sign * (step + 1)) * TEAM + ranks[slot]
            arrivals.append((copy, w_all.at[wrows(coming), lanes]))
        return arrivals

    ring = {}
    ring[0, 0] = ring_send(0, 0)
    scatter = {}
    for slot in range(1, TEAM):
        for k, ref in enumerate((wq_ref, wk_ref)):
            lanes = pl.ds(k * inner, inner)
            copy = remote(ref.at[:, cols(ranks[slot])], w_all.at[wrows(me), lanes], peers[slot])
            go(copy)
            scatter[slot, k] = (copy, w_all.at[wrows(peers[slot]), lanes])

    def lane_frequencies(shape, half_count):
        lane = lax.broadcasted_iota(jnp.int32, shape, 1) % half_count
        return jnp.exp(lane.astype(jnp.float32) * (-math.log(10000.0) / half_count))

    def sigma_rows(step):
        level = jnp.full((8, proj_ref.shape[0]), plan_ref[0, step], jnp.int32)
        return sigma_of(level)

    steps_sigma = [sigma_rows(step) for step in range(STEPS)]
    row_at = lax.broadcasted_iota(jnp.int32, steps_sigma[0].shape, 0)
    sigmas = jnp.zeros(steps_sigma[0].shape, jnp.float32)
    for step in range(STEPS):
        sigmas = jnp.where(row_at == step + 1, steps_sigma[step], sigmas)
    time_half = proj_ref.shape[0] // 2
    turns = 1000.0 * sigmas * lane_frequencies(sigmas.shape, time_half)
    first = lax.broadcasted_iota(jnp.int32, sigmas.shape, 1) < time_half
    features = jnp.where(first, jnp.cos(turns), jnp.sin(turns)).astype(jnp.bfloat16)
    mods[...] = jnp.dot(features, proj_ref[...], preferred_element_type=jnp.float32)

    def modulated(values, index):
        centred = values - jnp.mean(values, axis=-1, keepdims=True)
        variance = jnp.mean(centred * centred, axis=-1, keepdims=True)
        normed = centred * lax.rsqrt(variance + EPSILON)
        scale = mods[index : index + 1, width : 2 * width]
        return (normed * (1.0 + scale) + mods[index : index + 1, :width]).astype(jnp.bfloat16)

    def share(buffer, lead):
        own_view = buffer.at[lead + (rank,)]
        to_sib = remote(own_view, own_view, peers[1])
        to_far = remote(own_view, own_view, peers[2])
        go(to_far)
        go(to_sib)
        return (
            landing(to_sib, buffer.at[lead + (sib_rank,)]),
            landing(to_far, buffer.at[lead + (far_rank,)]),
        )

    def share_rest(buffer, lead, pending):
        from_sib, from_far = pending
        from_far.wait_recv()
        view = buffer.at[lead + (far_rank,)]
        forward = remote(view, view, peers[1])
        go(forward)
        from_sib.wait_recv()
        landing(forward, buffer.at[lead + (diag_rank,)]).wait_recv()

    def share_all(buffer, lead):
        waits = []
        view = buffer.at[lead + (rank,)]
        for slot in (2, 3, 1):
            copy = remote(view, view, peers[slot])
            go(copy)
            waits.append(landing(copy, buffer.at[lead + (ranks[slot],)]))
        return waits

    def pass_own(slot):
        for k in range(2):
            copy, view = scatter[slot, k]
            landing(copy, view).wait_recv()
        ring[0, slot] = ring_send(0, slot)

    def pass_on(step, slot):
        if step < half:
            for copy, view in ring[step - 1, slot]:
                landing(copy, view).wait_recv()
            ring[step, slot] = ring_send(step, slot)

    pass_own(1)
    latent[...] = noisy_ref[...].astype(jnp.float32)
    hid[0, pl.ds(rank, 1)] = modulated(latent[...], 1)[None]
    pending_noisy = share(hid, (0,))
    pass_on(1, 0)
    pass_own(2)
    pass_own(3)
    hid[1, pl.ds(rank, 1)] = modulated(clean_ref[...].astype(jnp.float32), 0)[None]
    pending_clean = share(hid, (1,))
    here = seg_ref[me]
    bias_lane = lax.broadcasted_iota(jnp.int32, (8, LAGS * rows), 1) // rows
    bias = jnp.zeros((8, LAGS * rows), jnp.float32)
    for distance in range(1, LAGS + 1):
        source = jnp.maximum(me - distance, 0)
        level = jnp.where(seg_ref[source] == here, 0.0, MASKED)
        level = jnp.where(lag_ref[0, distance - 1] == 1, level, MASKED)
        level = jnp.where(me >= distance, level, MASKED)
        bias = jnp.where(bias_lane == LAGS - distance, level, bias)
    bias_all[pl.ds(rank, 1)] = bias[None]
    pending_bias = share_all(bias_all, ())
    pass_on(1, 1)
    pass_on(1, 2)
    share_rest(hid, (0,), pending_noisy)
    pass_on(1, 3)
    share_rest(hid, (1,), pending_clean)
    pass_on(2, 0)
    for wait in pending_bias:
        wait.wait_recv()

    for s in range(TEAM):
        ctx_v[LAGS + s] = hid[1, s, :, cols(rank)]
    v_copy = remote(ctx_v.at[pl.ds(TEAM, LAGS)], ctx_v.at[pl.ds(0, LAGS)], later)
    go(v_copy)
    for slot in range(1, TEAM):
        pass_on(2, slot)

    half_count = HEAD_DIM // 2
    for s in range(TEAM):
        span_id = seg_ref[base + s]
        start = jnp.int32(0)
        for other in range(count):
            start = start + jnp.where(seg_ref[other] < span_id, 1, 0)
        place = (base + s - start) * rows
        shape = (rows, HEAD_DIM)
        position = (lax.broadcasted_iota(jnp.int32, shape, 0) + place).astype(jnp.float32)
        angles = position * lane_frequencies(shape, half_count)
        sine = jnp.sin(angles)
        front = lax.broadcasted_iota(jnp.int32, shape, 1) < half_count
        cos_ref[s * rows : (s + 1) * rows] = jnp.cos(angles)
        sin_ref[s * rows : (s + 1) * rows] = jnp.where(front, -sine, sine)

    for step in range(3, half):
        for slot in range(TEAM):
            pass_on(step, slot)
    for slot in range(TEAM):
        for copy, view in ring[half - 1, slot]:
            landing(copy, view).wait_recv()
    landing(v_copy, ctx_v.at[pl.ds(0, LAGS)]).wait_recv()

    all_rows = TEAM * rows

    def project(source, first, last, target):
        start = first
        while start < last:
            size = min(256, last - start)
            target[:, start - first : start - first + size] = jnp.dot(
                source, w_all[:, start : start + size], preferred_element_type=jnp.float32
            )
            start += size

    ones = jnp.ones((8, HEAD_DIM), jnp.float32)
    nt = (((1,), (1,)), ((), ()))

    def squares(values):
        folded = jnp.zeros((all_rows, HEAD_DIM), jnp.float32)
        for h in range(heads):
            head = values[:, h * HEAD_DIM : (h + 1) * HEAD_DIM]
            folded = folded + head * head
        return lax.dot_general(
            ones, folded, nt, precision=lax.Precision.HIGHEST,
            preferred_element_type=jnp.float32,
        )

    def row_scale(sums, index):
        pick = (lax.broadcasted_iota(jnp.int32, (8, 128), 0) == index).astype(jnp.float32)
        total = lax.dot_general(
            sums, pick, (((0,), (0,)), ((), ())), precision=lax.Precision.HIGHEST,
            preferred_element_type=jnp.float32,
        )
        return lax.rsqrt(total * (1.0 / width) + EPSILON)

    def turn(target, offset, gain_ref, h):
        lanes = slice(offset + h * HEAD_DIM, offset + (h + 1) * HEAD_DIM)
        gain = gain_ref[pl.ds(pl.multiple_of(rank * inner + h * HEAD_DIM, 128), HEAD_DIM)]
        value = target[:, lanes] * gain[None, :]
        rolled = pltpu.roll(value, HEAD_DIM // 2, 1)
        target[:, lanes] = value * cos_ref[...] + rolled * sin_ref[...]

    for step in range(STEPS):
        buffer = hid if step == 0 else hid2
        if step == 1:
            hid2[0, pl.ds(rank, 1)] = modulated(latent[...], 2)[None]
            share_rest(hid2, (0,), share(hid2, (0,)))
        row_kind = lax.broadcasted_iota(jnp.int32, (8, all_rows), 0)
        if step == 0:
            project(hid[1].reshape(all_rows, width), inner, 2 * inner, ck_raw)
            stat[STEPS, pl.ds(rank, 1)] = squares(ck_raw)[None]
            c_waits = share_all(stat, (STEPS,))
        project(buffer[0].reshape(all_rows, width), 0, 2 * inner, qk_raw)
        sums = jnp.where(
            row_kind == 0, squares(qk_raw.at[:, :inner]), squares(qk_raw.at[:, inner:])
        )
        stat[step, pl.ds(rank, 1)] = sums[None]
        waits = share_all(stat, (step,))

        def summed(index):
            return stat[index, 0] + stat[index, 1] + stat[index, 2] + stat[index, 3]

        if step == 0:
            for h in range(heads):
                turn(ck_raw, 0, kg_ref, h)
            for wait in c_waits:
                wait.wait_recv()
            c_scale = row_scale(summed(STEPS), 0)
            for h in range(heads):
                lanes = slice(h * HEAD_DIM, (h + 1) * HEAD_DIM)
                turned = (ck_raw[:, lanes] * c_scale).astype(jnp.bfloat16)
                ctx_k[LAGS : LAGS + TEAM, :, lanes] = turned.reshape(TEAM, rows, HEAD_DIM)
            k_copy = remote(ctx_k.at[pl.ds(TEAM, LAGS)], ctx_k.at[pl.ds(0, LAGS)], later)
            go(k_copy)
        for h in range(heads):
            turn(qk_raw, 0, qg_ref, h)
            turn(qk_raw, inner, kg_ref, h)
        for wait in waits:
            wait.wait_recv()
        total = summed(step)
        q_scale = row_scale(total, 0)
        k_scale = row_scale(total, 1)
        for h in range(heads):
            lanes = slice(h * HEAD_DIM, (h + 1) * HEAD_DIM)
            q_rows[:, lanes] = (qk_raw[:, lanes] * q_scale).astype(jnp.bfloat16)
            k_lanes = slice(inner + h * HEAD_DIM, inner + (h + 1) * HEAD_DIM)
            k_rows[:, lanes] = (qk_raw[:, k_lanes] * k_scale).astype(jnp.bfloat16)
        if step == 0:
            landing(k_copy, ctx_k.at[pl.ds(0, LAGS)]).wait_recv()
        waits = []
        for slot in (2, 3, 1, 0):
            s = ranks[slot]
            span = pl.ds(pl.multiple_of(s * rows, rows), rows)
            for h in range(heads):
                lanes = slice(h * HEAD_DIM, (h + 1) * HEAD_DIM)
                query = q_rows[span, lanes]
                keys = ctx_k[pl.ds(s, LAGS), :, lanes].reshape(LAGS * rows, HEAD_DIM)
                values = ctx_v[pl.ds(s, LAGS), :, lanes].reshape(LAGS * rows, HEAD_DIM)
                own_values = buffer[
                    0, s, :, pl.ds(pl.multiple_of(rank * inner + h * HEAD_DIM, 128), HEAD_DIM)
                ]
                near = lax.dot_general(
                    query, k_rows[span, lanes], nt, preferred_element_type=jnp.float32
                ) * HEAD_DIM ** (-0.5)
                past = lax.dot_general(
                    query, keys, nt, preferred_element_type=jnp.float32
                ) * HEAD_DIM ** (-0.5) + bias_all[s, 0:1, :]
                highest = jnp.maximum(
                    jnp.max(near, axis=-1, keepdims=True), jnp.max(past, axis=-1, keepdims=True)
                )
                near = jnp.exp(near - highest)
                past = jnp.exp(past - highest)
                inverse = 1.0 / (
                    jnp.sum(near, axis=-1, keepdims=True) + jnp.sum(past, axis=-1, keepdims=True)
                )
                mixed = jnp.dot(
                    (near * inverse).astype(jnp.bfloat16), own_values,
                    preferred_element_type=jnp.float32,
                ) + jnp.dot(
                    (past * inverse).astype(jnp.bfloat16), values,
                    preferred_element_type=jnp.float32,
                )
                mix_out[step, s, :, lanes] = mixed.astype(jnp.bfloat16)
            if slot:
                copy = remote(mix_out.at[step, s], mix.at[step, rank], peers[slot])
                go(copy)
                waits.append(landing(copy, mix.at[step, s]))
        mix[step, pl.ds(rank, 1)] = mix_out[step, pl.ds(rank, 1)]
        for wait in waits:
            wait.wait_recv()
        change = -steps_sigma[step][:1, :1]
        if step + 1 < STEPS:
            change = change + steps_sigma[step + 1][:1, :1]
        for r in range(TEAM):
            lanes = slice(r * inner, (r + 1) * inner)
            gate = mods[step + 1 : step + 2, 2 * width + r * inner : 2 * width + (r + 1) * inner]
            fresh = (
                latent[:, lanes] + (change * gate) * mix[step, r].astype(jnp.float32)
            ).astype(jnp.bfloat16)
            if step == STEPS - 1:
                out_ref[:, lanes] = fresh
            else:
                latent[:, lanes] = fresh.astype(jnp.float32)

    for copy in started:
        copy.wait_send()


def fused(noisy, clean, seg_ids, lag_mask, plan, w_query, w_key, time_proj, q_gain, k_gain):
    rows, width = noisy.shape
    inner = w_query.shape[1] // TEAM
    count = lax.axis_size("fsdp")
    vmem = pl.BlockSpec(memory_space=pltpu.VMEM)
    total = TEAM * rows
    bf16, f32 = jnp.bfloat16, jnp.float32
    copies = 96 + 4 * count
    return pl.pallas_call(
        functools.partial(fused_kernel, count),
        out_shape=jax.ShapeDtypeStruct(noisy.shape, bf16),
        in_specs=[pl.BlockSpec(memory_space=pltpu.SMEM)] * 3 + [vmem] * 7,
        out_specs=vmem,
        scratch_shapes=[
            pltpu.VMEM((width, 2 * inner), bf16),
            pltpu.VMEM((2, TEAM, rows, width), bf16),
            pltpu.VMEM((1, TEAM, rows, width), bf16),
            pltpu.VMEM((LAGS + TEAM, rows, inner), bf16),
            pltpu.VMEM((LAGS + TEAM, rows, inner), bf16),
            pltpu.VMEM((total, 2 * inner), f32),
            pltpu.VMEM((total, inner), f32),
            pltpu.VMEM((STEPS + 1, TEAM, 8, total), f32),
            pltpu.VMEM((STEPS, TEAM, rows, inner), bf16),
            pltpu.VMEM((STEPS, TEAM, rows, inner), bf16),
            pltpu.VMEM((rows, width), f32),
            pltpu.VMEM((8, 3 * width), f32),
            pltpu.VMEM((total, inner), bf16),
            pltpu.VMEM((total, inner), bf16),
            pltpu.VMEM((TEAM, 8, LAGS * rows), f32),
            pltpu.VMEM((total, HEAD_DIM), f32),
            pltpu.VMEM((total, HEAD_DIM), f32),
            pltpu.SemaphoreType.DMA((copies,)),
            pltpu.SemaphoreType.DMA((copies,)),
            pltpu.SemaphoreType.DMA((2,)),
        ],
        compiler_params=pltpu.CompilerParams(
            collective_id=0, has_side_effects=True, vmem_limit_bytes=48 * 1024 * 1024
        ),
    )(
        seg_ids, lag_mask, plan, noisy, clean, w_query, w_key, time_proj, q_gain, k_gain,
    )


def body(*arrays):
    part = arrays[5].shape[0]
    aligned = lax.axis_size("fsdp") % (2 * TEAM) == 0 and part % 16 == 0
    return (fused if aligned else local)(*arrays)


def solution(mesh):
    placed = (
        P(("pool", "fsdp"), None),
        P(("pool", "fsdp"), None),
        P("pool"),
        P(("pool", "fsdp"), None),
        P(("pool", "fsdp"), None),
        P("fsdp", None),
        P("fsdp", None),
        P(),
        P(),
        P(),
    )
    return jax.shard_map(
        body, mesh=mesh, in_specs=placed, out_specs=P(("pool", "fsdp"), None), check_vma=False
    )
```

```python
import functools
import math

import jax
import jax.numpy as jnp
from jax import lax
from jax.experimental import pallas as pl
from jax.experimental.pallas import tpu as pltpu
from jax.sharding import PartitionSpec as P

HEADS = 20
HEAD_DIM = 128
STEPS = 2
LAGS = 2
LEVELS = 1000


SIGMA_SHIFT = 5.0
EPSILON = 1e-06
MASKED = -1e30


def passed_along(value, axis, steps):
    count = lax.axis_size(axis)
    leading, last = (max(0, -steps), min(count, count - steps))
    return lax.ppermute(value, axis, [(source, source + steps) for source in range(leading, last)])


def sigma_of(levels):
    fraction = levels.astype(jnp.float32) / LEVELS
    return SIGMA_SHIFT * fraction / (1.0 + (SIGMA_SHIFT - 1.0) * fraction)


def frequencies(half_count):
    return jnp.exp(-math.log(10000.0) * jnp.arange(half_count, dtype=jnp.float32) / half_count)


def modulation(sigmas, time_proj):
    half_count = time_proj.shape[0] // 2
    angles = 1000.0 * sigmas[:, None] * frequencies(half_count)[None, :]
    features = jnp.concatenate([jnp.cos(angles), jnp.sin(angles)], axis=1).astype(jnp.bfloat16)
    return jnp.dot(features, time_proj, preferred_element_type=jnp.float32)[0]


def modulate(latent, mod_row, model_width):
    values = latent.astype(jnp.float32)
    centred = values - jnp.mean(values, axis=-1, keepdims=True)
    variance = jnp.mean(centred * centred, axis=-1, keepdims=True)
    normed = centred * lax.rsqrt(variance + EPSILON)
    return (normed * (1.0 + mod_row[model_width : 2 * model_width]) + mod_row[:model_width]).astype(
        jnp.bfloat16
    )


def normalize(values, gain):
    mean_square = jnp.mean(values * values, axis=-1, keepdims=True)
    return values * lax.rsqrt(mean_square + EPSILON) * gain


def rotate(values, positions):
    half_count = HEAD_DIM // 2
    split_heads = values.reshape(values.shape[:-1] + (HEADS, HEAD_DIM))
    angles = positions[..., None] * frequencies(half_count)
    cosine = jnp.cos(angles)[..., None, :]
    sine = jnp.sin(angles)[..., None, :]
    front = split_heads[..., :half_count]
    back = split_heads[..., half_count:]
    turned = jnp.concatenate([front * cosine - back * sine, front * sine + back * cosine], axis=-1)
    return turned.reshape(values.shape)


def attend(query_rows, key_rows, value_rows, usable):
    row_count = query_rows.shape[0]
    query_heads = query_rows.reshape(row_count, HEADS, HEAD_DIM)
    key_heads = key_rows.reshape(-1, HEADS, HEAD_DIM)
    value_heads = value_rows.reshape(-1, HEADS, HEAD_DIM)
    scores = jnp.einsum(
        "qhd,khd->hqk", query_heads, key_heads, preferred_element_type=jnp.float32
    ) * HEAD_DIM ** (-0.5)
    scores = jnp.where(usable[None, None, :], scores, MASKED)
    highest = jnp.max(scores, axis=-1, keepdims=True)
    expanded = jnp.exp(scores - highest)
    weights = (expanded / jnp.sum(expanded, axis=-1, keepdims=True)).astype(jnp.bfloat16)
    mixed = jnp.einsum("hqk,khd->qhd", weights, value_heads, preferred_element_type=jnp.float32)
    return mixed.reshape(row_count, HEADS * HEAD_DIM).astype(jnp.bfloat16)


def make_absorbers(noisy_hidden, context_hidden):

    def absorb_both(carry, pieces, offset):
        stored = tuple((piece_rows for piece_rows in pieces))
        query_sum = jnp.dot(noisy_hidden, pieces[0], preferred_element_type=jnp.float32)
        key_sum = jnp.dot(noisy_hidden, pieces[1], preferred_element_type=jnp.float32)
        ctxkey_sum = jnp.dot(context_hidden, pieces[1], preferred_element_type=jnp.float32)
        return (stored, (query_sum, key_sum, ctxkey_sum))

    def absorb_key(carry, piece, offset):
        buffer_rows, partials = carry
        stored = lax.dynamic_update_slice_in_dim(buffer_rows, piece, offset, 0)
        key_sum, ctxkey_sum = partials
        key_sum = key_sum + jnp.dot(noisy_hidden, piece, preferred_element_type=jnp.float32)
        ctxkey_sum = ctxkey_sum + jnp.dot(context_hidden, piece, preferred_element_type=jnp.float32)
        return (stored, (key_sum, ctxkey_sum))

    def absorb_query(carry, piece, offset):
        buffer_rows, query_sum = carry
        stored = lax.dynamic_update_slice_in_dim(buffer_rows, piece, offset, 0)
        query_sum = query_sum + jnp.dot(noisy_hidden, piece, preferred_element_type=jnp.float32)
        return (stored, query_sum)

    return (absorb_both, absorb_key, absorb_query)


def local(noisy, clean, seg_ids, lag_mask, plan, w_query, w_key, time_proj, q_gain, k_gain):
    row_count, model_width = noisy.shape
    inner_width = w_query.shape[1]
    span_index = lax.axis_index("fsdp")
    segment_start = jnp.sum((seg_ids < seg_ids[span_index]).astype(jnp.int32))
    span_place = span_index - segment_start
    positions = (span_place * row_count + jnp.arange(row_count, dtype=jnp.int32)).astype(
        jnp.float32
    )
    sigmas = [sigma_of(plan[0, level_index : level_index + 1]) for level_index in range(STEPS)] + [
        jnp.zeros((1,), jnp.float32)
    ]
    rest_mod = modulation(jnp.zeros((1,), jnp.float32), time_proj)
    step_mods = [modulation(sigmas[level_index], time_proj) for level_index in range(STEPS)]
    context_hidden = modulate(clean, rest_mod, model_width)
    noisy_hidden = modulate(noisy, step_mods[0], model_width)
    absorb_both, absorb_key, absorb_query = make_absorbers(noisy_hidden, context_hidden)
    empty_buffer = jnp.zeros((model_width, inner_width), jnp.bfloat16)
    empty_sum = jnp.zeros((row_count, inner_width), jnp.float32)
    buffers, partials = absorb_both(
        ((empty_buffer, empty_buffer), (empty_sum, empty_sum, empty_sum)),
        (
            lax.all_gather(w_query, "fsdp", axis=0, tiled=True),
            lax.all_gather(w_key, "fsdp", axis=0, tiled=True),
        ),
        jnp.int32(0),
    )
    full_query, full_key = buffers
    query_sum, key_sum, ctxkey_sum = partials
    context_key = rotate(normalize(ctxkey_sum, k_gain), positions).astype(jnp.bfloat16)
    context_pair = jnp.stack([context_key, context_hidden])
    received = [passed_along(context_pair, "fsdp", 1)]
    distance = 2
    received.append(passed_along(context_pair, "fsdp", distance))
    usable_parts = [jnp.ones((row_count,), jnp.int32) > 0]
    for distance in range(1, LAGS + 1):
        source = jnp.maximum(span_index - distance, 0)
        allowed = (
            (span_index >= distance)
            & (seg_ids[source] == seg_ids[span_index])
            & (lag_mask[0, distance - 1] == 1)
        )
        usable_parts.append(jnp.broadcast_to(allowed, (row_count,)))
    usable = jnp.concatenate(usable_parts)
    keys_context = jnp.concatenate([pair_rows[0] for pair_rows in received], axis=0)
    values_context = jnp.concatenate([pair_rows[1] for pair_rows in received], axis=0)
    latent = noisy
    for step_index in range(STEPS):
        if step_index == 0:
            hidden = noisy_hidden
            query_raw, key_raw = (query_sum, key_sum)
        else:
            hidden = modulate(latent, step_mods[step_index], model_width)
            query_raw = jnp.dot(hidden, full_query, preferred_element_type=jnp.float32)
            key_raw = jnp.dot(hidden, full_key, preferred_element_type=jnp.float32)
        query_rows = rotate(normalize(query_raw, q_gain), positions).astype(jnp.bfloat16)
        key_rows = rotate(normalize(key_raw, k_gain), positions).astype(jnp.bfloat16)
        mixed = attend(
            query_rows,
            jnp.concatenate([key_rows, keys_context], axis=0),
            jnp.concatenate([hidden, values_context], axis=0),
            usable,
        )
        sigma_change = sigmas[step_index + 1] - sigmas[step_index]
        factor = sigma_change * step_mods[step_index][2 * model_width :]
        latent = (latent.astype(jnp.float32) + factor[None, :] * mixed.astype(jnp.float32)).astype(
            jnp.bfloat16
        )
    return latent


TEAM = 4
MESH = pl.DeviceIdType.MESH


def fused_kernel(
    count, seg_ref, lag_ref, plan_ref, noisy_ref, clean_ref, wq_ref, wk_ref, proj_ref, qg_ref,
    kg_ref, out_ref,
    w_all, hid, hid2, ctx_k, ctx_v, qk_raw, ck_raw, stat, mix, mix_out, latent, mods, q_rows, k_rows,
    bias_all, cos_ref, sin_ref, send_sem, recv_sem, local_sem,
):
    rows, width = noisy_ref.shape
    part = wq_ref.shape[0]
    inner = wq_ref.shape[1] // TEAM
    heads = inner // HEAD_DIM
    groups = count // TEAM
    half = groups // 2
    me = lax.axis_index("fsdp")
    group = me // TEAM
    rank = me % TEAM
    sib_rank = rank + 1 - 2 * (rank % 2)
    far_rank = (rank + 2) % TEAM
    diag_rank = (sib_rank + 2) % TEAM
    ranks = [rank, sib_rank, far_rank, diag_rank]
    low = group % 2
    spot = group // 2 + low * (groups - 1 - 2 * (group // 2))

    def group_at(place):
        place = (place + 2 * groups) % groups
        upper = place // half
        return 2 * (place + upper * (groups - 1 - 2 * place)) + upper

    base = group * TEAM
    peers = [base + r for r in ranks]
    ring_next = group_at(spot + 1) * TEAM + rank
    ring_prev = group_at(spot - 1) * TEAM + rank
    later = ((group + 1) % groups) * TEAM + rank
    earlier = ((group + groups - 1) % groups) * TEAM + rank

    def cols(r):
        return pl.ds(pl.multiple_of(r * inner, 128), inner)

    def wrows(device):
        return pl.ds(pl.multiple_of(device * part, 16), part)

    barrier = pltpu.get_barrier_semaphore()
    friends = peers[1:] + [ring_next, ring_prev, later, earlier]
    for friend in friends:
        pl.semaphore_signal(barrier, inc=1, device_id={"fsdp": friend}, device_id_type=MESH)

    own = [
        pltpu.make_async_copy(
            ref.at[:, cols(rank)], w_all.at[wrows(me), pl.ds(k * inner, inner)], local_sem.at[k]
        )
        for k, ref in enumerate((wq_ref, wk_ref))
    ]
    for copy in own:
        copy.start()
    for copy in own:
        copy.wait()
    pl.semaphore_wait(barrier, len(friends))

    used = [0]
    started = []

    def remote(src, dst, target):
        index = used[0]
        used[0] += 1
        copy = pltpu.make_async_remote_copy(
            src_ref=src, dst_ref=dst, send_sem=send_sem.at[index], recv_sem=recv_sem.at[index],
            device_id={"fsdp": target}, device_id_type=MESH,
        )
        return copy, index

    def go(copy):
        copy[0].start()
        started.append(copy[0])

    def landing(copy, dst):
        return pltpu.make_async_remote_copy(
            src_ref=dst, dst_ref=dst, send_sem=send_sem.at[copy[1]],
            recv_sem=recv_sem.at[copy[1]], device_id={"fsdp": peers[1]}, device_id_type=MESH,
        )

    def ring_send(step, slot):
        arrivals = []
        for sign, target in ((1, ring_next), (-1, ring_prev)):
            lanes = pl.ds(0, 2 * inner)
            if step == half - 1:
                lanes = pl.ds(0, inner) if sign == 1 else pl.ds(inner, inner)
            source = group_at(spot - sign * step) * TEAM + ranks[slot]
            view = w_all.at[wrows(source), lanes]
            copy = remote(view, view, target)
            go(copy)
            coming = group_at(spot - sign * (step + 1)) * TEAM + ranks[slot]
            arrivals.append((copy, w_all.at[wrows(coming), lanes]))
        return arrivals

    ring = {}
    ring[0, 0] = ring_send(0, 0)
    scatter = {}
    for slot in range(1, TEAM):
        for k, ref in enumerate((wq_ref, wk_ref)):
            lanes = pl.ds(k * inner, inner)
            copy = remote(ref.at[:, cols(ranks[slot])], w_all.at[wrows(me), lanes], peers[slot])
            go(copy)
            scatter[slot, k] = (copy, w_all.at[wrows(peers[slot]), lanes])

    def lane_frequencies(shape, half_count):
        lane = lax.broadcasted_iota(jnp.int32, shape, 1) % half_count
        return jnp.exp(lane.astype(jnp.float32) * (-math.log(10000.0) / half_count))

    def sigma_rows(step):
        level = jnp.full((8, proj_ref.shape[0]), plan_ref[0, step], jnp.int32)
        return sigma_of(level)

    steps_sigma = [sigma_rows(step) for step in range(STEPS)]
    row_at = lax.broadcasted_iota(jnp.int32, steps_sigma[0].shape, 0)
    sigmas = jnp.zeros(steps_sigma[0].shape, jnp.float32)
    for step in range(STEPS):
        sigmas = jnp.where(row_at == step + 1, steps_sigma[step], sigmas)
    time_half = proj_ref.shape[0] // 2
    turns = 1000.0 * sigmas * lane_frequencies(sigmas.shape, time_half)
    first = lax.broadcasted_iota(jnp.int32, sigmas.shape, 1) < time_half
    features = jnp.where(first, jnp.cos(turns), jnp.sin(turns)).astype(jnp.bfloat16)
    mods[...] = jnp.dot(features, proj_ref[...], preferred_element_type=jnp.float32)

    def modulated(values, index):
        centred = values - jnp.mean(values, axis=-1, keepdims=True)
        variance = jnp.mean(centred * centred, axis=-1, keepdims=True)
        normed = centred * lax.rsqrt(variance + EPSILON)
        scale = mods[index : index + 1, width : 2 * width]
        return (normed * (1.0 + scale) + mods[index : index + 1, :width]).astype(jnp.bfloat16)

    def share(buffer, lead, lanes=slice(None)):
        own_view = buffer.at[lead + (rank, slice(None), lanes)]
        to_sib = remote(own_view, own_view, peers[1])
        to_far = remote(own_view, own_view, peers[2])
        go(to_far)
        go(to_sib)
        return (
            landing(to_sib, buffer.at[lead + (sib_rank, slice(None), lanes)]),
            landing(to_far, buffer.at[lead + (far_rank, slice(None), lanes)]),
        )

    def share_rest(buffer, lead, pending, lanes=slice(None)):
        from_sib, from_far = pending
        from_far.wait_recv()
        view = buffer.at[lead + (far_rank, slice(None), lanes)]
        forward = remote(view, view, peers[1])
        go(forward)
        from_sib.wait_recv()
        landing(forward, buffer.at[lead + (diag_rank, slice(None), lanes)]).wait_recv()

    def share_all(buffer, lead):
        waits = []
        view = buffer.at[lead + (rank,)]
        for slot in (2, 3, 1):
            copy = remote(view, view, peers[slot])
            go(copy)
            waits.append(landing(copy, buffer.at[lead + (ranks[slot],)]))
        return waits

    def pass_own(slot):
        for k in range(2):
            copy, view = scatter[slot, k]
            landing(copy, view).wait_recv()
        ring[0, slot] = ring_send(0, slot)

    def pass_on(step, slot):
        if step < half:
            for copy, view in ring[step - 1, slot]:
                landing(copy, view).wait_recv()
            ring[step, slot] = ring_send(step, slot)

    pass_own(1)
    latent[...] = noisy_ref[...].astype(jnp.float32)
    hid[0, pl.ds(rank, 1)] = modulated(latent[...], 1)[None]
    pending_noisy = share(hid, (0,))
    pass_on(1, 0)
    pass_own(2)
    pass_own(3)
    hid[1, pl.ds(rank, 1)] = modulated(clean_ref[...].astype(jnp.float32), 0)[None]
    pending_clean = share(hid, (1,))
    here = seg_ref[me]
    bias_lane = lax.broadcasted_iota(jnp.int32, (8, LAGS * rows), 1) // rows
    bias = jnp.zeros((8, LAGS * rows), jnp.float32)
    for distance in range(1, LAGS + 1):
        source = jnp.maximum(me - distance, 0)
        level = jnp.where(seg_ref[source] == here, 0.0, MASKED)
        level = jnp.where(lag_ref[0, distance - 1] == 1, level, MASKED)
        level = jnp.where(me >= distance, level, MASKED)
        bias = jnp.where(bias_lane == LAGS - distance, level, bias)
    bias_all[pl.ds(rank, 1)] = bias[None]
    pending_bias = share_all(bias_all, ())
    pass_on(1, 1)
    pass_on(1, 2)
    share_rest(hid, (0,), pending_noisy)
    pass_on(1, 3)
    share_rest(hid, (1,), pending_clean)
    pass_on(2, 0)
    for wait in pending_bias:
        wait.wait_recv()

    for s in range(TEAM):
        ctx_v[LAGS + s] = hid[1, s, :, cols(rank)]
    v_copy = remote(ctx_v.at[pl.ds(TEAM, LAGS)], ctx_v.at[pl.ds(0, LAGS)], later)
    go(v_copy)
    for slot in range(1, TEAM):
        pass_on(2, slot)

    half_count = HEAD_DIM // 2
    for s in range(TEAM):
        span_id = seg_ref[base + s]
        start = jnp.int32(0)
        for other in range(count):
            start = start + jnp.where(seg_ref[other] < span_id, 1, 0)
        place = (base + s - start) * rows
        shape = (rows, HEAD_DIM)
        position = (lax.broadcasted_iota(jnp.int32, shape, 0) + place).astype(jnp.float32)
        angles = position * lane_frequencies(shape, half_count)
        sine = jnp.sin(angles)
        front = lax.broadcasted_iota(jnp.int32, shape, 1) < half_count
        cos_ref[s * rows : (s + 1) * rows] = jnp.cos(angles)
        sin_ref[s * rows : (s + 1) * rows] = jnp.where(front, -sine, sine)

    for step in range(3, half):
        for slot in range(TEAM):
            pass_on(step, slot)
    all_rows = TEAM * rows
    farthest = group_at(spot + half) // 2

    def project(buffer, kind, start, size, first, last, target, fresh):
        source = buffer[kind, :, :, pl.ds(start, size)].reshape(all_rows, size)
        left = first
        while left < last:
            block = min(256, last - left)
            product = jnp.dot(
                source, w_all[pl.ds(start, size), left : left + block],
                preferred_element_type=jnp.float32,
            )
            into = slice(left - first, left - first + block)
            target[:, into] = product if fresh else target[:, into] + product
            left += block

    def project_pair(pair, fresh):
        size = 2 * TEAM * part
        start = pl.multiple_of(pair * size, 128)
        project(hid, 1, start, size, inner, 2 * inner, ck_raw, fresh)
        project(hid, 0, start, size, 0, 2 * inner, qk_raw, fresh)

    for index in range(1, half):
        project_pair((farthest + index) % half, index == 1)
    for slot in range(TEAM):
        for copy, view in ring[half - 1, slot]:
            landing(copy, view).wait_recv()
    project_pair(farthest, half == 1)
    landing(v_copy, ctx_v.at[pl.ds(0, LAGS)]).wait_recv()


    ones = jnp.ones((8, HEAD_DIM), jnp.float32)
    nt = (((1,), (1,)), ((), ()))

    def squares(values):
        folded = jnp.zeros((all_rows, HEAD_DIM), jnp.float32)
        for h in range(heads):
            head = values[:, h * HEAD_DIM : (h + 1) * HEAD_DIM]
            folded = folded + head * head
        return lax.dot_general(
            ones, folded, nt, precision=lax.Precision.HIGHEST,
            preferred_element_type=jnp.float32,
        )

    def row_scale(sums, index):
        pick = (lax.broadcasted_iota(jnp.int32, (8, 128), 0) == index).astype(jnp.float32)
        total = lax.dot_general(
            sums, pick, (((0,), (0,)), ((), ())), precision=lax.Precision.HIGHEST,
            preferred_element_type=jnp.float32,
        )
        return lax.rsqrt(total * (1.0 / width) + EPSILON)

    def turn(target, offset, gain_ref, h):
        lanes = slice(offset + h * HEAD_DIM, offset + (h + 1) * HEAD_DIM)
        gain = gain_ref[pl.ds(pl.multiple_of(rank * inner + h * HEAD_DIM, 128), HEAD_DIM)]
        value = target[:, lanes] * gain[None, :]
        rolled = pltpu.roll(value, HEAD_DIM // 2, 1)
        target[:, lanes] = value * cos_ref[...] + rolled * sin_ref[...]

    for step in range(STEPS):
        buffer = hid if step == 0 else hid2
        if step == 1:
            hid2[0, pl.ds(rank, 1)] = modulated(latent[...], 2)[None]
            chunk = 2 * inner
            starts = range(0, width, chunk)
            pending = [share(hid2, (0,), pl.ds(start, chunk)) for start in starts]
            for start, flight in zip(starts, pending):
                share_rest(hid2, (0,), flight, pl.ds(start, chunk))
                project(hid2, 0, start, chunk, 0, 2 * inner, qk_raw, start == 0)
        row_kind = lax.broadcasted_iota(jnp.int32, (8, all_rows), 0)
        if step == 0:
            stat[STEPS, pl.ds(rank, 1)] = squares(ck_raw)[None]
            c_waits = share_all(stat, (STEPS,))
        sums = jnp.where(
            row_kind == 0, squares(qk_raw.at[:, :inner]), squares(qk_raw.at[:, inner:])
        )
        stat[step, pl.ds(rank, 1)] = sums[None]
        waits = share_all(stat, (step,))

        def summed(index):
            return stat[index, 0] + stat[index, 1] + stat[index, 2] + stat[index, 3]

        if step == 0:
            for h in range(heads):
                turn(ck_raw, 0, kg_ref, h)
            for wait in c_waits:
                wait.wait_recv()
            c_scale = row_scale(summed(STEPS), 0)
            for h in range(heads):
                lanes = slice(h * HEAD_DIM, (h + 1) * HEAD_DIM)
                turned = (ck_raw[:, lanes] * c_scale).astype(jnp.bfloat16)
                ctx_k[LAGS : LAGS + TEAM, :, lanes] = turned.reshape(TEAM, rows, HEAD_DIM)
            k_copy = remote(ctx_k.at[pl.ds(TEAM, LAGS)], ctx_k.at[pl.ds(0, LAGS)], later)
            go(k_copy)
        for h in range(heads):
            turn(qk_raw, 0, qg_ref, h)
            turn(qk_raw, inner, kg_ref, h)
        for wait in waits:
            wait.wait_recv()
        total = summed(step)
        q_scale = row_scale(total, 0)
        k_scale = row_scale(total, 1)
        for h in range(heads):
            lanes = slice(h * HEAD_DIM, (h + 1) * HEAD_DIM)
            q_rows[:, lanes] = (qk_raw[:, lanes] * q_scale).astype(jnp.bfloat16)
            k_lanes = slice(inner + h * HEAD_DIM, inner + (h + 1) * HEAD_DIM)
            k_rows[:, lanes] = (qk_raw[:, k_lanes] * k_scale).astype(jnp.bfloat16)
        if step == 0:
            landing(k_copy, ctx_k.at[pl.ds(0, LAGS)]).wait_recv()
        waits = []
        for slot in (2, 3, 1, 0):
            s = ranks[slot]
            span = pl.ds(pl.multiple_of(s * rows, rows), rows)
            for h in range(heads):
                lanes = slice(h * HEAD_DIM, (h + 1) * HEAD_DIM)
                query = q_rows[span, lanes]
                keys = ctx_k[pl.ds(s, LAGS), :, lanes].reshape(LAGS * rows, HEAD_DIM)
                values = ctx_v[pl.ds(s, LAGS), :, lanes].reshape(LAGS * rows, HEAD_DIM)
                own_values = buffer[
                    0, s, :, pl.ds(pl.multiple_of(rank * inner + h * HEAD_DIM, 128), HEAD_DIM)
                ]
                near = lax.dot_general(
                    query, k_rows[span, lanes], nt, preferred_element_type=jnp.float32
                ) * HEAD_DIM ** (-0.5)
                past = lax.dot_general(
                    query, keys, nt, preferred_element_type=jnp.float32
                ) * HEAD_DIM ** (-0.5) + bias_all[s, 0:1, :]
                highest = jnp.maximum(
                    jnp.max(near, axis=-1, keepdims=True), jnp.max(past, axis=-1, keepdims=True)
                )
                near = jnp.exp(near - highest)
                past = jnp.exp(past - highest)
                inverse = 1.0 / (
                    jnp.sum(near, axis=-1, keepdims=True) + jnp.sum(past, axis=-1, keepdims=True)
                )
                mixed = jnp.dot(
                    (near * inverse).astype(jnp.bfloat16), own_values,
                    preferred_element_type=jnp.float32,
                ) + jnp.dot(
                    (past * inverse).astype(jnp.bfloat16), values,
                    preferred_element_type=jnp.float32,
                )
                mix_out[step, s, :, lanes] = mixed.astype(jnp.bfloat16)
            if slot:
                copy = remote(mix_out.at[step, s], mix.at[step, rank], peers[slot])
                go(copy)
                waits.append(landing(copy, mix.at[step, s]))
        mix[step, pl.ds(rank, 1)] = mix_out[step, pl.ds(rank, 1)]
        for wait in waits:
            wait.wait_recv()
        change = -steps_sigma[step][:1, :1]
        if step + 1 < STEPS:
            change = change + steps_sigma[step + 1][:1, :1]
        for r in range(TEAM):
            lanes = slice(r * inner, (r + 1) * inner)
            gate = mods[step + 1 : step + 2, 2 * width + r * inner : 2 * width + (r + 1) * inner]
            fresh = (
                latent[:, lanes] + (change * gate) * mix[step, r].astype(jnp.float32)
            ).astype(jnp.bfloat16)
            if step == STEPS - 1:
                out_ref[:, lanes] = fresh
            else:
                latent[:, lanes] = fresh.astype(jnp.float32)

    for copy in started:
        copy.wait_send()


def fused(noisy, clean, seg_ids, lag_mask, plan, w_query, w_key, time_proj, q_gain, k_gain):
    rows, width = noisy.shape
    inner = w_query.shape[1] // TEAM
    count = lax.axis_size("fsdp")
    vmem = pl.BlockSpec(memory_space=pltpu.VMEM)
    total = TEAM * rows
    bf16, f32 = jnp.bfloat16, jnp.float32
    copies = 96 + 4 * count
    return pl.pallas_call(
        functools.partial(fused_kernel, count),
        out_shape=jax.ShapeDtypeStruct(noisy.shape, bf16),
        in_specs=[pl.BlockSpec(memory_space=pltpu.SMEM)] * 3 + [vmem] * 7,
        out_specs=vmem,
        scratch_shapes=[
            pltpu.VMEM((width, 2 * inner), bf16),
            pltpu.VMEM((2, TEAM, rows, width), bf16),
            pltpu.VMEM((1, TEAM, rows, width), bf16),
            pltpu.VMEM((LAGS + TEAM, rows, inner), bf16),
            pltpu.VMEM((LAGS + TEAM, rows, inner), bf16),
            pltpu.VMEM((total, 2 * inner), f32),
            pltpu.VMEM((total, inner), f32),
            pltpu.VMEM((STEPS + 1, TEAM, 8, total), f32),
            pltpu.VMEM((STEPS, TEAM, rows, inner), bf16),
            pltpu.VMEM((STEPS, TEAM, rows, inner), bf16),
            pltpu.VMEM((rows, width), f32),
            pltpu.VMEM((8, 3 * width), f32),
            pltpu.VMEM((total, inner), bf16),
            pltpu.VMEM((total, inner), bf16),
            pltpu.VMEM((TEAM, 8, LAGS * rows), f32),
            pltpu.VMEM((total, HEAD_DIM), f32),
            pltpu.VMEM((total, HEAD_DIM), f32),
            pltpu.SemaphoreType.DMA((copies,)),
            pltpu.SemaphoreType.DMA((copies,)),
            pltpu.SemaphoreType.DMA((2,)),
        ],
        compiler_params=pltpu.CompilerParams(
            collective_id=0, has_side_effects=True, vmem_limit_bytes=48 * 1024 * 1024
        ),
    )(
        seg_ids, lag_mask, plan, noisy, clean, w_query, w_key, time_proj, q_gain, k_gain,
    )


def body(*arrays):
    part = arrays[5].shape[0]
    aligned = lax.axis_size("fsdp") % (2 * TEAM) == 0 and part % 16 == 0
    return (fused if aligned else local)(*arrays)


def solution(mesh):
    placed = (
        P(("pool", "fsdp"), None),
        P(("pool", "fsdp"), None),
        P("pool"),
        P(("pool", "fsdp"), None),
        P(("pool", "fsdp"), None),
        P("fsdp", None),
        P("fsdp", None),
        P(),
        P(),
        P(),
    )
    return jax.shard_map(
        body, mesh=mesh, in_specs=placed, out_specs=P(("pool", "fsdp"), None), check_vma=False
    )
```

```python
import functools
import math

import jax
import jax.numpy as jnp
from jax import lax
from jax.experimental import pallas as pl
from jax.experimental.pallas import tpu as pltpu
from jax.sharding import PartitionSpec as P

HEADS = 20
HEAD_DIM = 128
STEPS = 2
LAGS = 2
LEVELS = 1000


SIGMA_SHIFT = 5.0
EPSILON = 1e-06
MASKED = -1e30


def passed_along(value, axis, steps):
    count = lax.axis_size(axis)
    leading, last = (max(0, -steps), min(count, count - steps))
    return lax.ppermute(value, axis, [(source, source + steps) for source in range(leading, last)])


def sigma_of(levels):
    fraction = levels.astype(jnp.float32) / LEVELS
    return SIGMA_SHIFT * fraction / (1.0 + (SIGMA_SHIFT - 1.0) * fraction)


def frequencies(half_count):
    return jnp.exp(-math.log(10000.0) * jnp.arange(half_count, dtype=jnp.float32) / half_count)


def modulation(sigmas, time_proj):
    half_count = time_proj.shape[0] // 2
    angles = 1000.0 * sigmas[:, None] * frequencies(half_count)[None, :]
    features = jnp.concatenate([jnp.cos(angles), jnp.sin(angles)], axis=1).astype(jnp.bfloat16)
    return jnp.dot(features, time_proj, preferred_element_type=jnp.float32)[0]


def modulate(latent, mod_row, model_width):
    values = latent.astype(jnp.float32)
    centred = values - jnp.mean(values, axis=-1, keepdims=True)
    variance = jnp.mean(centred * centred, axis=-1, keepdims=True)
    normed = centred * lax.rsqrt(variance + EPSILON)
    return (normed * (1.0 + mod_row[model_width : 2 * model_width]) + mod_row[:model_width]).astype(
        jnp.bfloat16
    )


def normalize(values, gain):
    mean_square = jnp.mean(values * values, axis=-1, keepdims=True)
    return values * lax.rsqrt(mean_square + EPSILON) * gain


def rotate(values, positions):
    half_count = HEAD_DIM // 2
    split_heads = values.reshape(values.shape[:-1] + (HEADS, HEAD_DIM))
    angles = positions[..., None] * frequencies(half_count)
    cosine = jnp.cos(angles)[..., None, :]
    sine = jnp.sin(angles)[..., None, :]
    front = split_heads[..., :half_count]
    back = split_heads[..., half_count:]
    turned = jnp.concatenate([front * cosine - back * sine, front * sine + back * cosine], axis=-1)
    return turned.reshape(values.shape)


def attend(query_rows, key_rows, value_rows, usable):
    row_count = query_rows.shape[0]
    query_heads = query_rows.reshape(row_count, HEADS, HEAD_DIM)
    key_heads = key_rows.reshape(-1, HEADS, HEAD_DIM)
    value_heads = value_rows.reshape(-1, HEADS, HEAD_DIM)
    scores = jnp.einsum(
        "qhd,khd->hqk", query_heads, key_heads, preferred_element_type=jnp.float32
    ) * HEAD_DIM ** (-0.5)
    scores = jnp.where(usable[None, None, :], scores, MASKED)
    highest = jnp.max(scores, axis=-1, keepdims=True)
    expanded = jnp.exp(scores - highest)
    weights = (expanded / jnp.sum(expanded, axis=-1, keepdims=True)).astype(jnp.bfloat16)
    mixed = jnp.einsum("hqk,khd->qhd", weights, value_heads, preferred_element_type=jnp.float32)
    return mixed.reshape(row_count, HEADS * HEAD_DIM).astype(jnp.bfloat16)


def make_absorbers(noisy_hidden, context_hidden):

    def absorb_both(carry, pieces, offset):
        stored = tuple((piece_rows for piece_rows in pieces))
        query_sum = jnp.dot(noisy_hidden, pieces[0], preferred_element_type=jnp.float32)
        key_sum = jnp.dot(noisy_hidden, pieces[1], preferred_element_type=jnp.float32)
        ctxkey_sum = jnp.dot(context_hidden, pieces[1], preferred_element_type=jnp.float32)
        return (stored, (query_sum, key_sum, ctxkey_sum))

    def absorb_key(carry, piece, offset):
        buffer_rows, partials = carry
        stored = lax.dynamic_update_slice_in_dim(buffer_rows, piece, offset, 0)
        key_sum, ctxkey_sum = partials
        key_sum = key_sum + jnp.dot(noisy_hidden, piece, preferred_element_type=jnp.float32)
        ctxkey_sum = ctxkey_sum + jnp.dot(context_hidden, piece, preferred_element_type=jnp.float32)
        return (stored, (key_sum, ctxkey_sum))

    def absorb_query(carry, piece, offset):
        buffer_rows, query_sum = carry
        stored = lax.dynamic_update_slice_in_dim(buffer_rows, piece, offset, 0)
        query_sum = query_sum + jnp.dot(noisy_hidden, piece, preferred_element_type=jnp.float32)
        return (stored, query_sum)

    return (absorb_both, absorb_key, absorb_query)


def local(noisy, clean, seg_ids, lag_mask, plan, w_query, w_key, time_proj, q_gain, k_gain):
    row_count, model_width = noisy.shape
    inner_width = w_query.shape[1]
    span_index = lax.axis_index("fsdp")
    segment_start = jnp.sum((seg_ids < seg_ids[span_index]).astype(jnp.int32))
    span_place = span_index - segment_start
    positions = (span_place * row_count + jnp.arange(row_count, dtype=jnp.int32)).astype(
        jnp.float32
    )
    sigmas = [sigma_of(plan[0, level_index : level_index + 1]) for level_index in range(STEPS)] + [
        jnp.zeros((1,), jnp.float32)
    ]
    rest_mod = modulation(jnp.zeros((1,), jnp.float32), time_proj)
    step_mods = [modulation(sigmas[level_index], time_proj) for level_index in range(STEPS)]
    context_hidden = modulate(clean, rest_mod, model_width)
    noisy_hidden = modulate(noisy, step_mods[0], model_width)
    absorb_both, absorb_key, absorb_query = make_absorbers(noisy_hidden, context_hidden)
    empty_buffer = jnp.zeros((model_width, inner_width), jnp.bfloat16)
    empty_sum = jnp.zeros((row_count, inner_width), jnp.float32)
    buffers, partials = absorb_both(
        ((empty_buffer, empty_buffer), (empty_sum, empty_sum, empty_sum)),
        (
            lax.all_gather(w_query, "fsdp", axis=0, tiled=True),
            lax.all_gather(w_key, "fsdp", axis=0, tiled=True),
        ),
        jnp.int32(0),
    )
    full_query, full_key = buffers
    query_sum, key_sum, ctxkey_sum = partials
    context_key = rotate(normalize(ctxkey_sum, k_gain), positions).astype(jnp.bfloat16)
    context_pair = jnp.stack([context_key, context_hidden])
    received = [passed_along(context_pair, "fsdp", 1)]
    distance = 2
    received.append(passed_along(context_pair, "fsdp", distance))
    usable_parts = [jnp.ones((row_count,), jnp.int32) > 0]
    for distance in range(1, LAGS + 1):
        source = jnp.maximum(span_index - distance, 0)
        allowed = (
            (span_index >= distance)
            & (seg_ids[source] == seg_ids[span_index])
            & (lag_mask[0, distance - 1] == 1)
        )
        usable_parts.append(jnp.broadcast_to(allowed, (row_count,)))
    usable = jnp.concatenate(usable_parts)
    keys_context = jnp.concatenate([pair_rows[0] for pair_rows in received], axis=0)
    values_context = jnp.concatenate([pair_rows[1] for pair_rows in received], axis=0)
    latent = noisy
    for step_index in range(STEPS):
        if step_index == 0:
            hidden = noisy_hidden
            query_raw, key_raw = (query_sum, key_sum)
        else:
            hidden = modulate(latent, step_mods[step_index], model_width)
            query_raw = jnp.dot(hidden, full_query, preferred_element_type=jnp.float32)
            key_raw = jnp.dot(hidden, full_key, preferred_element_type=jnp.float32)
        query_rows = rotate(normalize(query_raw, q_gain), positions).astype(jnp.bfloat16)
        key_rows = rotate(normalize(key_raw, k_gain), positions).astype(jnp.bfloat16)
        mixed = attend(
            query_rows,
            jnp.concatenate([key_rows, keys_context], axis=0),
            jnp.concatenate([hidden, values_context], axis=0),
            usable,
        )
        sigma_change = sigmas[step_index + 1] - sigmas[step_index]
        factor = sigma_change * step_mods[step_index][2 * model_width :]
        latent = (latent.astype(jnp.float32) + factor[None, :] * mixed.astype(jnp.float32)).astype(
            jnp.bfloat16
        )
    return latent


TEAM = 4
MESH = pl.DeviceIdType.MESH


def fused_kernel(
    count, seg_ref, lag_ref, plan_ref, noisy_ref, clean_ref, wq_ref, wk_ref, proj_ref, qg_ref,
    kg_ref, out_ref,
    w_all, hid, hid2, ctx_k, ctx_v, qk_raw, ck_raw, stat, mix, mix_out, latent, mods, q_rows, k_rows,
    bias_all, cos_ref, sin_ref, send_sem, recv_sem, local_sem,
):
    rows, width = noisy_ref.shape
    part = wq_ref.shape[0]
    inner = wq_ref.shape[1] // TEAM
    heads = inner // HEAD_DIM
    groups = count // TEAM
    half = groups // 2
    me = lax.axis_index("fsdp")
    group = me // TEAM
    rank = me % TEAM
    sib_rank = rank + 1 - 2 * (rank % 2)
    far_rank = (rank + 2) % TEAM
    diag_rank = (sib_rank + 2) % TEAM
    ranks = [rank, sib_rank, far_rank, diag_rank]
    low = group % 2
    spot = group // 2 + low * (groups - 1 - 2 * (group // 2))

    def group_at(place):
        place = (place + 2 * groups) % groups
        upper = place // half
        return 2 * (place + upper * (groups - 1 - 2 * place)) + upper

    base = group * TEAM
    peers = [base + r for r in ranks]
    ring_next = group_at(spot + 1) * TEAM + rank
    ring_prev = group_at(spot - 1) * TEAM + rank
    later = ((group + 1) % groups) * TEAM + rank
    earlier = ((group + groups - 1) % groups) * TEAM + rank

    def cols(r):
        return pl.ds(pl.multiple_of(r * inner, 128), inner)

    def wrows(device):
        return pl.ds(pl.multiple_of(device * part, 16), part)

    barrier = pltpu.get_barrier_semaphore()
    friends = peers[1:] + [ring_next, ring_prev, later, earlier]
    for friend in friends:
        pl.semaphore_signal(barrier, inc=1, device_id={"fsdp": friend}, device_id_type=MESH)

    own = [
        pltpu.make_async_copy(
            ref.at[:, cols(rank)], w_all.at[wrows(me), pl.ds(k * inner, inner)], local_sem.at[k]
        )
        for k, ref in enumerate((wq_ref, wk_ref))
    ]
    for copy in own:
        copy.start()
    for copy in own:
        copy.wait()
    pl.semaphore_wait(barrier, len(friends))

    used = [0]
    started = []

    def remote(src, dst, target):
        index = used[0]
        used[0] += 1
        copy = pltpu.make_async_remote_copy(
            src_ref=src, dst_ref=dst, send_sem=send_sem.at[index], recv_sem=recv_sem.at[index],
            device_id={"fsdp": target}, device_id_type=MESH,
        )
        return copy, index

    def go(copy):
        copy[0].start()
        started.append(copy[0])

    def landing(copy, dst):
        return pltpu.make_async_remote_copy(
            src_ref=dst, dst_ref=dst, send_sem=send_sem.at[copy[1]],
            recv_sem=recv_sem.at[copy[1]], device_id={"fsdp": peers[1]}, device_id_type=MESH,
        )

    def ring_send(step, slot):
        arrivals = []
        for sign, target in ((1, ring_next), (-1, ring_prev)):
            lanes = pl.ds(0, 2 * inner)
            if step == half - 1:
                lanes = pl.ds(0, inner) if sign == 1 else pl.ds(inner, inner)
            source = group_at(spot - sign * step) * TEAM + ranks[slot]
            view = w_all.at[wrows(source), lanes]
            copy = remote(view, view, target)
            go(copy)
            coming = group_at(spot - sign * (step + 1)) * TEAM + ranks[slot]
            arrivals.append((copy, w_all.at[wrows(coming), lanes]))
        return arrivals

    ring = {}
    ring[0, 0] = ring_send(0, 0)
    scatter = {}
    for slot in range(1, TEAM):
        for k, ref in enumerate((wq_ref, wk_ref)):
            lanes = pl.ds(k * inner, inner)
            copy = remote(ref.at[:, cols(ranks[slot])], w_all.at[wrows(me), lanes], peers[slot])
            go(copy)
            scatter[slot, k] = (copy, w_all.at[wrows(peers[slot]), lanes])

    def lane_frequencies(shape, half_count):
        lane = lax.broadcasted_iota(jnp.int32, shape, 1) % half_count
        return jnp.exp(lane.astype(jnp.float32) * (-math.log(10000.0) / half_count))

    def sigma_rows(step):
        level = jnp.full((8, proj_ref.shape[0]), plan_ref[0, step], jnp.int32)
        return sigma_of(level)

    steps_sigma = [sigma_rows(step) for step in range(STEPS)]
    row_at = lax.broadcasted_iota(jnp.int32, steps_sigma[0].shape, 0)
    sigmas = jnp.zeros(steps_sigma[0].shape, jnp.float32)
    for step in range(STEPS):
        sigmas = jnp.where(row_at == step + 1, steps_sigma[step], sigmas)
    time_half = proj_ref.shape[0] // 2
    turns = 1000.0 * sigmas * lane_frequencies(sigmas.shape, time_half)
    first = lax.broadcasted_iota(jnp.int32, sigmas.shape, 1) < time_half
    features = jnp.where(first, jnp.cos(turns), jnp.sin(turns)).astype(jnp.bfloat16)
    mods[...] = jnp.dot(features, proj_ref[...], preferred_element_type=jnp.float32)

    def modulated(values, index):
        centred = values - jnp.mean(values, axis=-1, keepdims=True)
        variance = jnp.mean(centred * centred, axis=-1, keepdims=True)
        normed = centred * lax.rsqrt(variance + EPSILON)
        scale = mods[index : index + 1, width : 2 * width]
        return (normed * (1.0 + scale) + mods[index : index + 1, :width]).astype(jnp.bfloat16)

    def share(buffer, lead, lanes=slice(None)):
        own_view = buffer.at[lead + (rank, slice(None), lanes)]
        to_sib = remote(own_view, own_view, peers[1])
        to_far = remote(own_view, own_view, peers[2])
        go(to_far)
        go(to_sib)
        return (
            landing(to_sib, buffer.at[lead + (sib_rank, slice(None), lanes)]),
            landing(to_far, buffer.at[lead + (far_rank, slice(None), lanes)]),
        )

    def share_rest(buffer, lead, pending, lanes=slice(None)):
        from_sib, from_far = pending
        from_far.wait_recv()
        view = buffer.at[lead + (far_rank, slice(None), lanes)]
        forward = remote(view, view, peers[1])
        go(forward)
        from_sib.wait_recv()
        landing(forward, buffer.at[lead + (diag_rank, slice(None), lanes)]).wait_recv()

    def share_all(buffer, lead):
        waits = []
        view = buffer.at[lead + (rank,)]
        for slot in (2, 3, 1):
            copy = remote(view, view, peers[slot])
            go(copy)
            waits.append(landing(copy, buffer.at[lead + (ranks[slot],)]))
        return waits

    def pass_own(slot):
        for k in range(2):
            copy, view = scatter[slot, k]
            landing(copy, view).wait_recv()
        ring[0, slot] = ring_send(0, slot)

    def pass_on(step, slot):
        if step < half:
            for copy, view in ring[step - 1, slot]:
                landing(copy, view).wait_recv()
            ring[step, slot] = ring_send(step, slot)

    pass_own(1)
    latent[...] = noisy_ref[...].astype(jnp.float32)
    hid[0, pl.ds(rank, 1)] = modulated(latent[...], 1)[None]
    pending_noisy = share(hid, (0,))
    pass_on(1, 0)
    pass_own(2)
    pass_own(3)
    hid[1, pl.ds(rank, 1)] = modulated(clean_ref[...].astype(jnp.float32), 0)[None]
    pending_clean = share(hid, (1,))
    here = seg_ref[me]
    bias_lane = lax.broadcasted_iota(jnp.int32, (8, LAGS * rows), 1) // rows
    bias = jnp.zeros((8, LAGS * rows), jnp.float32)
    for distance in range(1, LAGS + 1):
        source = jnp.maximum(me - distance, 0)
        level = jnp.where(seg_ref[source] == here, 0.0, MASKED)
        level = jnp.where(lag_ref[0, distance - 1] == 1, level, MASKED)
        level = jnp.where(me >= distance, level, MASKED)
        bias = jnp.where(bias_lane == LAGS - distance, level, bias)
    bias_all[pl.ds(rank, 1)] = bias[None]
    pending_bias = share_all(bias_all, ())
    pass_on(1, 1)
    pass_on(1, 2)
    share_rest(hid, (0,), pending_noisy)
    pass_on(1, 3)
    share_rest(hid, (1,), pending_clean)
    pass_on(2, 0)
    for wait in pending_bias:
        wait.wait_recv()

    for s in range(TEAM):
        ctx_v[LAGS + s] = hid[1, s, :, cols(rank)]
    v_copy = remote(ctx_v.at[pl.ds(TEAM, LAGS)], ctx_v.at[pl.ds(0, LAGS)], later)
    go(v_copy)
    for slot in range(1, TEAM):
        pass_on(2, slot)

    half_count = HEAD_DIM // 2
    for s in range(TEAM):
        span_id = seg_ref[base + s]
        start = jnp.int32(0)
        for other in range(count):
            start = start + jnp.where(seg_ref[other] < span_id, 1, 0)
        place = (base + s - start) * rows
        shape = (rows, HEAD_DIM)
        position = (lax.broadcasted_iota(jnp.int32, shape, 0) + place).astype(jnp.float32)
        angles = position * lane_frequencies(shape, half_count)
        sine = jnp.sin(angles)
        front = lax.broadcasted_iota(jnp.int32, shape, 1) < half_count
        cos_ref[s * rows : (s + 1) * rows] = jnp.cos(angles)
        sin_ref[s * rows : (s + 1) * rows] = jnp.where(front, -sine, sine)

    for step in range(3, half):
        for slot in range(TEAM):
            pass_on(step, slot)
    all_rows = TEAM * rows
    farthest = group_at(spot + half) // 2

    def project(buffer, kind, start, size, first, last, target, fresh):
        source = buffer[kind, :, :, pl.ds(start, size)].reshape(all_rows, size)
        left = first
        while left < last:
            block = min(256, last - left)
            product = jnp.dot(
                source, w_all[pl.ds(start, size), left : left + block],
                preferred_element_type=jnp.float32,
            )
            into = slice(left - first, left - first + block)
            target[:, into] = product if fresh else target[:, into] + product
            left += block

    def project_pair(pair, fresh):
        size = 2 * TEAM * part
        start = pl.multiple_of(pair * size, 128)
        project(hid, 1, start, size, inner, 2 * inner, ck_raw, fresh)
        project(hid, 0, start, size, 0, 2 * inner, qk_raw, fresh)

    for index in range(1, half):
        project_pair((farthest + index) % half, index == 1)
    for slot in range(TEAM):
        for copy, view in ring[half - 1, slot]:
            landing(copy, view).wait_recv()
    project_pair(farthest, half == 1)
    landing(v_copy, ctx_v.at[pl.ds(0, LAGS)]).wait_recv()


    ones = jnp.ones((8, HEAD_DIM), jnp.float32)
    nt = (((1,), (1,)), ((), ()))

    def squares(values):
        folded = jnp.zeros((all_rows, HEAD_DIM), jnp.float32)
        for h in range(heads):
            head = values[:, h * HEAD_DIM : (h + 1) * HEAD_DIM]
            folded = folded + head * head
        return lax.dot_general(
            ones, folded, nt, precision=lax.Precision.HIGHEST,
            preferred_element_type=jnp.float32,
        )

    def row_scale(sums, index):
        pick = (lax.broadcasted_iota(jnp.int32, (8, 128), 0) == index).astype(jnp.float32)
        total = lax.dot_general(
            sums, pick, (((0,), (0,)), ((), ())), precision=lax.Precision.HIGHEST,
            preferred_element_type=jnp.float32,
        )
        return lax.rsqrt(total * (1.0 / width) + EPSILON)

    def turn(target, offset, gain_ref, h):
        lanes = slice(offset + h * HEAD_DIM, offset + (h + 1) * HEAD_DIM)
        gain = gain_ref[pl.ds(pl.multiple_of(rank * inner + h * HEAD_DIM, 128), HEAD_DIM)]
        value = target[:, lanes] * gain[None, :]
        rolled = pltpu.roll(value, HEAD_DIM // 2, 1)
        target[:, lanes] = value * cos_ref[...] + rolled * sin_ref[...]

    for step in range(STEPS):
        buffer = hid if step == 0 else hid2
        if step == 1:
            hid2[0, pl.ds(rank, 1)] = modulated(latent[...], 2)[None]
            chunk = 2 * inner
            starts = range(0, width, chunk)
            pending = [share(hid2, (0,), pl.ds(start, chunk)) for start in starts]
            for start, flight in zip(starts, pending):
                share_rest(hid2, (0,), flight, pl.ds(start, chunk))
                project(hid2, 0, start, chunk, 0, 2 * inner, qk_raw, start == 0)
        row_kind = lax.broadcasted_iota(jnp.int32, (8, all_rows), 0)
        if step == 0:
            stat[STEPS, pl.ds(rank, 1)] = squares(ck_raw)[None]
            c_waits = share_all(stat, (STEPS,))
        sums = jnp.where(
            row_kind == 0, squares(qk_raw.at[:, :inner]), squares(qk_raw.at[:, inner:])
        )
        stat[step, pl.ds(rank, 1)] = sums[None]
        waits = share_all(stat, (step,))

        def summed(index):
            return stat[index, 0] + stat[index, 1] + stat[index, 2] + stat[index, 3]

        if step == 0:
            for h in range(heads):
                turn(ck_raw, 0, kg_ref, h)
            for wait in c_waits:
                wait.wait_recv()
            c_scale = row_scale(summed(STEPS), 0)
            for h in range(heads):
                lanes = slice(h * HEAD_DIM, (h + 1) * HEAD_DIM)
                turned = (ck_raw[:, lanes] * c_scale).astype(jnp.bfloat16)
                ctx_k[LAGS : LAGS + TEAM, :, lanes] = turned.reshape(TEAM, rows, HEAD_DIM)
            k_copy = remote(ctx_k.at[pl.ds(TEAM, LAGS)], ctx_k.at[pl.ds(0, LAGS)], later)
            go(k_copy)
        for h in range(heads):
            turn(qk_raw, 0, qg_ref, h)
            turn(qk_raw, inner, kg_ref, h)
        for wait in waits:
            wait.wait_recv()
        total = summed(step)
        q_scale = row_scale(total, 0)
        k_scale = row_scale(total, 1)
        for h in range(heads):
            lanes = slice(h * HEAD_DIM, (h + 1) * HEAD_DIM)
            q_rows[:, lanes] = (qk_raw[:, lanes] * q_scale).astype(jnp.bfloat16)
            k_lanes = slice(inner + h * HEAD_DIM, inner + (h + 1) * HEAD_DIM)
            k_rows[:, lanes] = (qk_raw[:, k_lanes] * k_scale).astype(jnp.bfloat16)
        if step == 0:
            landing(k_copy, ctx_k.at[pl.ds(0, LAGS)]).wait_recv()
        waits = []
        for slot in (2, 3, 1, 0):
            s = ranks[slot]
            span = pl.ds(pl.multiple_of(s * rows, rows), rows)
            head_lanes = [slice(h * HEAD_DIM, (h + 1) * HEAD_DIM) for h in range(heads)]
            nears, pasts = [], []
            for lanes in head_lanes:
                query = q_rows[span, lanes]
                keys = ctx_k[pl.ds(s, LAGS), :, lanes].reshape(LAGS * rows, HEAD_DIM)
                nears.append(lax.dot_general(
                    query, k_rows[span, lanes], nt, preferred_element_type=jnp.float32
                ))
                pasts.append(lax.dot_general(
                    query, keys, nt, preferred_element_type=jnp.float32
                ))
            near = jnp.concatenate(nears, axis=0) * HEAD_DIM ** (-0.5)
            past = jnp.concatenate(pasts, axis=0) * HEAD_DIM ** (-0.5) + bias_all[s, 0:1, :]
            highest = jnp.maximum(
                jnp.max(near, axis=-1, keepdims=True), jnp.max(past, axis=-1, keepdims=True)
            )
            near = jnp.exp(near - highest)
            past = jnp.exp(past - highest)
            inverse = 1.0 / (
                jnp.sum(near, axis=-1, keepdims=True) + jnp.sum(past, axis=-1, keepdims=True)
            )
            near = (near * inverse).astype(jnp.bfloat16)
            past = (past * inverse).astype(jnp.bfloat16)
            outs = []
            for h, lanes in enumerate(head_lanes):
                values = ctx_v[pl.ds(s, LAGS), :, lanes].reshape(LAGS * rows, HEAD_DIM)
                own_values = buffer[
                    0, s, :, pl.ds(pl.multiple_of(rank * inner + h * HEAD_DIM, 128), HEAD_DIM)
                ]
                block = slice(h * rows, (h + 1) * rows)
                outs.append(jnp.dot(
                    near[block], own_values, preferred_element_type=jnp.float32
                ) + jnp.dot(past[block], values, preferred_element_type=jnp.float32))
            for lanes, mixed in zip(head_lanes, outs):
                mix_out[step, s, :, lanes] = mixed.astype(jnp.bfloat16)
            if slot:
                copy = remote(mix_out.at[step, s], mix.at[step, rank], peers[slot])
                go(copy)
                waits.append(landing(copy, mix.at[step, s]))
        mix[step, pl.ds(rank, 1)] = mix_out[step, pl.ds(rank, 1)]
        for wait in waits:
            wait.wait_recv()
        change = -steps_sigma[step][:1, :1]
        if step + 1 < STEPS:
            change = change + steps_sigma[step + 1][:1, :1]
        for r in range(TEAM):
            lanes = slice(r * inner, (r + 1) * inner)
            gate = mods[step + 1 : step + 2, 2 * width + r * inner : 2 * width + (r + 1) * inner]
            fresh = (
                latent[:, lanes] + (change * gate) * mix[step, r].astype(jnp.float32)
            ).astype(jnp.bfloat16)
            if step == STEPS - 1:
                out_ref[:, lanes] = fresh
            else:
                latent[:, lanes] = fresh.astype(jnp.float32)

    for copy in started:
        copy.wait_send()


def fused(noisy, clean, seg_ids, lag_mask, plan, w_query, w_key, time_proj, q_gain, k_gain):
    rows, width = noisy.shape
    inner = w_query.shape[1] // TEAM
    count = lax.axis_size("fsdp")
    vmem = pl.BlockSpec(memory_space=pltpu.VMEM)
    total = TEAM * rows
    bf16, f32 = jnp.bfloat16, jnp.float32
    copies = 96 + 4 * count
    return pl.pallas_call(
        functools.partial(fused_kernel, count),
        out_shape=jax.ShapeDtypeStruct(noisy.shape, bf16),
        in_specs=[pl.BlockSpec(memory_space=pltpu.SMEM)] * 3 + [vmem] * 7,
        out_specs=vmem,
        scratch_shapes=[
            pltpu.VMEM((width, 2 * inner), bf16),
            pltpu.VMEM((2, TEAM, rows, width), bf16),
            pltpu.VMEM((1, TEAM, rows, width), bf16),
            pltpu.VMEM((LAGS + TEAM, rows, inner), bf16),
            pltpu.VMEM((LAGS + TEAM, rows, inner), bf16),
            pltpu.VMEM((total, 2 * inner), f32),
            pltpu.VMEM((total, inner), f32),
            pltpu.VMEM((STEPS + 1, TEAM, 8, total), f32),
            pltpu.VMEM((STEPS, TEAM, rows, inner), bf16),
            pltpu.VMEM((STEPS, TEAM, rows, inner), bf16),
            pltpu.VMEM((rows, width), f32),
            pltpu.VMEM((8, 3 * width), f32),
            pltpu.VMEM((total, inner), bf16),
            pltpu.VMEM((total, inner), bf16),
            pltpu.VMEM((TEAM, 8, LAGS * rows), f32),
            pltpu.VMEM((total, HEAD_DIM), f32),
            pltpu.VMEM((total, HEAD_DIM), f32),
            pltpu.SemaphoreType.DMA((copies,)),
            pltpu.SemaphoreType.DMA((copies,)),
            pltpu.SemaphoreType.DMA((2,)),
        ],
        compiler_params=pltpu.CompilerParams(
            collective_id=0, has_side_effects=True, vmem_limit_bytes=48 * 1024 * 1024
        ),
    )(
        seg_ids, lag_mask, plan, noisy, clean, w_query, w_key, time_proj, q_gain, k_gain,
    )


def body(*arrays):
    part = arrays[5].shape[0]
    aligned = lax.axis_size("fsdp") % (2 * TEAM) == 0 and part % 16 == 0
    return (fused if aligned else local)(*arrays)


def solution(mesh):
    placed = (
        P(("pool", "fsdp"), None),
        P(("pool", "fsdp"), None),
        P("pool"),
        P(("pool", "fsdp"), None),
        P(("pool", "fsdp"), None),
        P("fsdp", None),
        P("fsdp", None),
        P(),
        P(),
        P(),
    )
    return jax.shard_map(
        body, mesh=mesh, in_specs=placed, out_specs=P(("pool", "fsdp"), None), check_vma=False
    )
```
